256 devices in a mesh: gx: 32 (over y_lo, z, core), gy: 8 (over x, y_hi).
Axes of the slice: x: 4, y: 4 (y_hi: 2, y_lo: 2; y = y_hi * 2 + y_lo), z: 8, core: 2. Of those that a mesh axis runs over, the one named last changes fastest.
Arguments:
- occupancy: int32 [2, 1024, 1024], P(None, 'gx', 'gy'), may hold values from 0 to 1, as said below
- colour: int32 [2, 1024, 1024], P(None, 'gx', 'gy'), may hold values 0 or 1
- hop_direction: int32 [2, 2, 1024, 1024], P(None, None, 'gx', 'gy'), may hold values from 0 to 3
- barrier: float32 [2, 1024, 1024], P(None, 'gx', 'gy'), may hold values from -4 to 4
Outputs:
- strain: float32 [3, 2, 1024, 1024], P(None, None, 'gx', 'gy')
- composition: float32 [2, 1024, 1024], P(None, 'gx', 'gy')
The draws below stay inside these ranges and needn't reach their ends.
Inputs may be any that keep to these rules, and one draw needn't show every extreme that they name: `occupancy`: 1 for a Ge atom, 0 for Si.
All inputs are finite; a program needn't handle non-finite values. No bound on the sum of `colour` on one device may be relied on, other than what follows from the above.
Results may differ from the reference program's by a relative error of at most 0.00011.
Values sent between devices are 32-bit elements; how exact they have to be, the bound alone decides.
A program may use at most 128 MiB of HBM per device.

```python
import math
import jax
import jax.numpy as jnp

NX = 1024
NY = 1024
LAYERS = 2
ITERS = 3
SECTIONS = 2


def draw_occupancy(key, part):
    key_x, key_y, key_sites = jax.random.split(key, 3)
    shift_x = jax.random.randint(key_x, (LAYERS, 1, 1), 0, NX)
    shift_y = jax.random.randint(key_y, (LAYERS, 1, 1), 0, NY)
    row_index = jnp.arange(NX, dtype=jnp.int32)[None, :, None]
    col_index = jnp.arange(NY, dtype=jnp.int32)[None, None, :]
    tent_x = jnp.abs((row_index + shift_x) % NX - NX // 2)
    tent_y = jnp.abs((col_index + shift_y) % NY - NY // 2)
    threshold = 150 + 700 * tent_x * tent_y // (NX // 2 * (NY // 2))
    site_draws = jax.random.randint(key_sites, (LAYERS, NX, NY), 0, 1000)
    return (site_draws < threshold).astype(jnp.int32)


def plant(array, key, least, top_value):
    longest = array.shape.index(max(array.shape))
    spots = []
    for shift in (0, 1):
        where = [jax.random.randint(jax.random.fold_in(key, axis), (), 0, length) for axis, length in enumerate(array.shape)]
        where[longest] = (where[longest] + shift) % array.shape[longest]
        spots.append(tuple(where))
    return array.at[spots[0]].set(least).at[spots[1]].set(top_value)


def levels(rng, shape, shards, low, high):
    level, own = 1.0, jax.random.fold_in(rng, 6)
    for dim, shards_of in shards:
        draws = jnp.exp(jax.random.uniform(jax.random.fold_in(own, dim), (shards_of,), jnp.float32, low / len(shards), high / len(shards)))
        level = level * jnp.repeat(draws, shape[dim] // shards_of).reshape([-1 if axis == dim else 1 for axis in range(len(shape))])
    return level


def centred(own_key, shape, scale, bound, cuts=(), kind=jnp.bfloat16):
    entries = jax.random.normal(own_key, shape, jnp.float32) * scale
    if len(cuts) > 0:
        entries = levels(own_key, shape, cuts, -0.22, 0.18) * entries
    return jnp.clip(entries, min=-bound, max=bound).astype(kind)


def setup_inputs(seed: int = 0) -> dict:
    key_of = jax.random.split(jax.random.key(seed), 5)
    occupancy = draw_occupancy(jax.random.fold_in(key_of[4], 71), 0)
    colour = plant((jax.random.randint(key_of[1], (LAYERS, NX, NY), 0, 2) < 1).astype(jnp.int32), jax.random.fold_in(key_of[1], 1), 0, 1)
    hop_direction = plant(jax.random.randint(key_of[2], (SECTIONS, LAYERS, NX, NY), 0, 4), jax.random.fold_in(key_of[2], 1), 0, 3).astype(jnp.int32)
    barrier = centred(key_of[3], (LAYERS, NX, NY), 1.0, 4.0, ((1, 32), (2, 8)), jnp.float32)
    return dict(occupancy=occupancy, colour=colour, hop_direction=hop_direction, barrier=barrier)


lame_silicon = 1.2
lame_germanium = 0.9
shear_silicon = 1.0
shear_germanium = 0.8
lame_medium = 1.05
shear_medium = 0.9
elastic_weight = 2.0
bond_energy = 0.7
base_rate = 1.0


def local_stress(strain, fraction):
    lame_field = lame_silicon + (lame_germanium - lame_silicon) * fraction
    shear_field = shear_silicon + (shear_germanium - shear_silicon) * fraction
    excess_xx = strain[0] - fraction
    excess_yy = strain[1] - fraction
    trace_part = lame_field * (excess_xx + excess_yy)
    return jnp.stack([trace_part + 2.0 * shear_field * excess_xx,
                      trace_part + 2.0 * shear_field * excess_yy,
                      2.0 * shear_field * strain[2]])


def energy_density(strain, fraction):
    stress = local_stress(strain, fraction)
    return 0.5 * (stress[0] * (strain[0] - fraction) + stress[1] * (strain[1] - fraction)
                  + 2.0 * stress[2] * strain[2])


def wave_numbers(points, first_index, length_of):
    index = first_index + jnp.arange(length_of, dtype=jnp.int32)
    signed = jnp.where(index < points // 2, index, index - points)
    return signed.astype(jnp.float32) * (2.0 * math.pi / points)


def green_apply(part_xx, part_yy, part_xy, wave_x, wave_y):
    ratio = (lame_medium + shear_medium) / (lame_medium + 2.0 * shear_medium)
    squared = wave_x * wave_x + wave_y * wave_y
    positive = squared > 0
    inverse_sq = jnp.where(positive, 1.0 / jnp.where(positive, squared, 1.0), 0.0)
    trac_x = wave_x * part_xx + wave_y * part_xy
    trac_y = wave_x * part_xy + wave_y * part_yy
    along = ratio * (wave_x * trac_x + wave_y * trac_y) * inverse_sq
    disp_x = (trac_x - wave_x * along) * inverse_sq / shear_medium
    disp_y = (trac_y - wave_y * along) * inverse_sq / shear_medium
    return (wave_x * disp_x, wave_y * disp_y, 0.5 * (wave_x * disp_y + wave_y * disp_x))


def hop_flux(composition, above, below, before, after, energy, barrier, colour, direction, section_index):
    neighbours = above + below + before + after
    rate = jax.nn.sigmoid(barrier + elastic_weight * energy - bond_energy * neighbours + base_rate)
    target = jnp.where(direction == 0, below, jnp.where(direction == 1, above,
                                                       jnp.where(direction == 2, after, before)))
    flux = jnp.where(colour == section_index, rate * composition * (1.0 - target), 0.0)
    return flux, [jnp.where(direction == number, flux, 0.0) for number in range(4)]


def reference(occupancy, colour, hop_direction, barrier):
    fraction = occupancy.astype(jnp.float32)
    wave_x = wave_numbers(NX, 0, NX)[:, None]
    wave_y = wave_numbers(NY, 0, NY)[None, :]
    strain = jnp.zeros((3, LAYERS, NX, NY), jnp.float32)
    for sweep_index in range(ITERS):
        stress = local_stress(strain, fraction)
        spectrum = jnp.fft.fft2(stress)
        mapped = green_apply(spectrum[0], spectrum[1], spectrum[2], wave_x, wave_y)
        change = jnp.real(jnp.fft.ifft2(jnp.stack(mapped))).astype(jnp.float32)
        strain = strain - change
    energy = energy_density(strain, fraction)
    composition = fraction
    for section_index in range(SECTIONS):
        above = jnp.roll(composition, 1, axis=1)
        below = jnp.roll(composition, -1, axis=1)
        before = jnp.roll(composition, 1, axis=2)
        after = jnp.roll(composition, -1, axis=2)
        flux, parted = hop_flux(composition, above, below, before, after, energy, barrier,
                                colour, hop_direction[section_index], section_index)
        inflow = (jnp.roll(parted[0], 1, axis=1) + jnp.roll(parted[1], -1, axis=1)
                  + jnp.roll(parted[2], 1, axis=2) + jnp.roll(parted[3], -1, axis=2))
        composition = composition - flux + inflow
    return strain, composition
```

```python
import math

import jax
import jax.numpy as jnp
import ml_dtypes
import numpy as np
from jax import lax
from jax.experimental import pallas as pl
from jax.experimental.pallas import tpu as pltpu
from jax.sharding import PartitionSpec as P

MESH = pl.DeviceIdType.MESH
F32 = jnp.float32
BF16 = jnp.bfloat16

ITERS = 3
SECTIONS = 2
GX, GY = 32, 8
DEVICES = GX * GY
POINTS = 1024
ROWS, COLS = POINTS // GX, POINTS // GY
STATIC = 10

lame_silicon = 1.2
lame_germanium = 0.9
shear_silicon = 1.0
shear_germanium = 0.8
lame_medium = 1.05
shear_medium = 0.9
elastic_weight = 2.0
bond_energy = 0.7
base_rate = 1.0


def split(values):
    high = values.astype(ml_dtypes.bfloat16)
    return high, (values - high.astype(np.float64)).astype(ml_dtypes.bfloat16)


def tables():
    index = np.arange(256)
    angle = 2 * np.pi * (np.outer(index, index) % 256) / 256
    dft_high, dft_low = split(np.concatenate([np.cos(angle), np.sin(angle)], 1))
    lane = np.arange(128)
    angle = 2 * np.pi * np.outer(index, lane % 4) / POINTS
    turn_x = np.stack([np.cos(angle), np.sin(angle)]).astype(np.float32)
    angle = 2 * np.pi * np.outer(np.arange(64) // 16, index) / POINTS
    turn_y = np.stack([np.cos(angle), np.sin(angle)]).astype(np.float32)
    part, freq, comp, quad = lane // 64, lane // 16 % 4, lane // 4 % 4, lane % 4
    turns = np.outer(quad, quad) % 4
    cos4, sin4 = np.array([1, 0, -1, 0])[turns], np.array([0, 1, 0, -1])[turns]
    same_freq = freq[:, None] == freq[None, :]
    same_part = part[:, None] == part[None, :]
    to_real = part[None, :] == 0
    used = (comp[None, :] < 3) & same_freq
    forward = np.where(same_part, cos4, np.where(to_real, sin4, -sin4))
    forward4 = np.concatenate([forward * (used & (comp[:, None] == c)) for c in range(3)], 1)
    inverse = np.where(same_part, cos4, np.where(to_real, -sin4, sin4))
    inverse = inverse * (used & (comp[:, None] == comp[None, :]))
    turned = np.concatenate([-inverse[:, 64:], inverse[:, :64]], 1)
    inverse4 = np.concatenate([inverse, turned], 1)
    return (
        dft_high,
        dft_low,
        turn_x,
        turn_y,
        np.concatenate([forward4, forward4], 0).astype(ml_dtypes.bfloat16),
        np.concatenate([inverse4, inverse4], 0).astype(ml_dtypes.bfloat16),
    )


def halves(values):
    high = values.astype(BF16)
    return high, (values - high.astype(F32)).astype(BF16)


def dot(left, right, dims):
    return lax.dot_general(left, right, (dims, ((), ())), preferred_element_type=F32)


def table_left(dft, values, dims):
    high, low = halves(values)
    return dot(dft[0][...], high, dims) + dot(dft[0][...], low, dims) + dot(dft[1][...], high, dims)


def table_right(dft, values, dims):
    high, low = halves(values)
    return dot(high, dft[0][...], dims) + dot(low, dft[0][...], dims) + dot(high, dft[1][...], dims)


def green_tables(device, green):
    shape = (256, 128)
    lane = lax.broadcasted_iota(jnp.int32, shape, 1)
    comp = lax.rem(lane // 4, 4)
    index_x = lax.broadcasted_iota(jnp.int32, shape, 0) + 256 * lax.rem(lane, 4)
    index_y = 4 * device + lax.rem(lane // 16, 4)
    unit = 2.0 * math.pi / POINTS
    a = jnp.where(index_x < POINTS // 2, index_x, index_x - POINTS).astype(F32) * unit
    b = jnp.where(index_y < POINTS // 2, index_y, index_y - POINTS).astype(F32) * unit
    ratio = (lame_medium + shear_medium) / (lame_medium + 2.0 * shear_medium)
    squared = a * a + b * b
    positive = squared > 0
    inverse_sq = jnp.where(positive, 1.0 / jnp.where(positive, squared, 1.0), 0.0)
    base = inverse_sq * (-1.0 / (shear_medium * POINTS * POINTS))
    edge_x = (index_x == POINTS // 2).astype(F32)
    edge_y = (index_y == POINTS // 2).astype(F32)
    odd = base * (1.0 - jnp.abs(edge_x - edge_y))
    aa, bb, ab = a * a, b * b, a * b
    xx_xx = (aa - ratio * aa * aa * inverse_sq) * base
    yy_yy = (bb - ratio * bb * bb * inverse_sq) * base
    xx_yy = -ratio * aa * bb * inverse_sq * base
    xx_xy = (ab - 2.0 * ratio * aa * ab * inverse_sq) * odd
    yy_xy = (ab - 2.0 * ratio * bb * ab * inverse_sq) * odd
    xy_xy = 0.5 * (aa + bb - 4.0 * ratio * aa * bb * inverse_sq) * base

    def pick(first, second, third):
        return jnp.where(
            comp == 0, first, jnp.where(comp == 1, second, jnp.where(comp == 2, third, 0.0))
        )

    green[0] = pick(xx_xx, xx_yy, 0.5 * xx_xy)
    green[1] = pick(xx_yy, yy_yy, 0.5 * yy_xy)
    green[2] = pick(xx_xy, yy_xy, xy_xy)


def spectral(received, dft, turn_x, forward4, inverse4, green):
    sign = jnp.where(lax.broadcasted_iota(jnp.int32, (256, 128), 1) < 64, 1.0, -1.0)
    swapped = pltpu.roll(received, 64, 1) * sign
    both = jnp.concatenate(
        [
            jnp.concatenate([received, swapped], 1),
            jnp.concatenate([swapped, -received], 1),
        ],
        0,
    )
    first = table_left(dft, both, ((1,), (0,)))
    turned = turn_x[0] * first[:, :128] + turn_x[1] * first[:, 128:]
    spread = dot(jnp.concatenate(halves(turned), 1), forward4[...], ((1,), (0,)))
    mapped = (
        green[0] * spread[:, :128] + green[1] * spread[:, 128:256] + green[2] * spread[:, 256:]
    )
    back = dot(jnp.concatenate(halves(mapped), 1), inverse4[...], ((1,), (0,)))
    plain, crossed = back[:, :128], back[:, 128:]
    values = turn_x[0] * plain + turn_x[1] * crossed
    crossed = turn_x[0] * crossed - turn_x[1] * plain
    return table_left(dft, jnp.concatenate([values, crossed], 0), ((1,), (0,)))


def four(parts, sign):
    (r0, r1, r2, r3), (i0, i1, i2, i3) = parts
    er, ei, dr, di = r0 + r2, i0 + i2, r0 - r2, i0 - i2
    fr, fi, gr, gi = r1 + r3, i1 + i3, r1 - r3, i1 - i3
    up_r, up_i = dr - gi, di + gr
    down_r, down_i = dr + gi, di - gr
    if sign < 0:
        up_r, up_i, down_r, down_i = down_r, down_i, up_r, up_i
    return (er + fr, up_r, er - fr, down_r), (ei + fi, up_i, ei - fi, down_i)


def forward_y(stress, dft, turn_y):
    parts = [[field[:, 256 * a : 256 * a + 256] for a in range(4)] for field in stress]
    real, imag = (jnp.concatenate(list(part), 0) for part in four(parts, -1))
    turned_real = turn_y[0] * real + turn_y[1] * imag
    turned_imag = turn_y[0] * imag - turn_y[1] * real
    rows = jnp.concatenate(
        [
            jnp.concatenate([turned_real, turned_imag], 1),
            jnp.concatenate([turned_imag, -turned_real], 1),
        ],
        0,
    )
    return table_left(dft, rows, ((1,), (1,)))


def inverse_y(received, dft, turn_y):
    across = received.T
    real, imag = across[:64], across[64:]
    rows = jnp.concatenate(
        [jnp.concatenate([real, -imag], 1), jnp.concatenate([imag, real], 1)], 0
    )
    both = table_right(dft, rows, ((1,), (1,)))
    real, imag = both[:64], both[64:]
    turned_real = turn_y[0] * real - turn_y[1] * imag
    turned_imag = turn_y[0] * imag + turn_y[1] * real
    parts = [
        [part[16 * j : 16 * j + 16] for j in range(4)] for part in (turned_real, turned_imag)
    ]
    return [jnp.concatenate(list(part), 1) for part in four(parts, 1)]


def local_stress(normal, shear, fraction):
    lame_field = lame_silicon + (lame_germanium - lame_silicon) * fraction
    shear_field = 2.0 * (shear_silicon + (shear_germanium - shear_silicon) * fraction)
    excess = normal - fraction
    trace = excess + pltpu.roll(excess, 4, 0)
    return lame_field * trace + shear_field * excess, shear_field * shear, excess


def ring(steps, size):
    return min(steps % size, -steps % size)


def kernel(
    occupancy,
    colour,
    direction,
    barrier,
    dft_high,
    dft_low,
    turn_x,
    turn_y,
    forward4,
    inverse4,
    strain_out,
    composition_out,
    green,
    normal,
    shear,
    fraction_pencil,
    packed,
    landed,
    fraction_sent,
    fraction_got,
    static,
    static_y,
    static_x,
    static_corner,
    strain_sent,
    strain_got,
    energy_sent,
    energy_got,
    gather_sem,
    send_sem,
    recv_sem,
    fraction_send,
    fraction_recv,
    static_send,
    static_recv,
    last_send,
    last_recv,
    edge_send,
    edge_recv,
):
    gx, gy = lax.axis_index("gx"), lax.axis_index("gy")
    me = gx * GY + gy
    dft = (dft_high, dft_low)
    z, core = lax.rem(gx // 2, 8), lax.rem(gx, 2)
    x, y = gy // 2, lax.rem(gy, 2) * 2 + gx // 16

    places = sorted(
        [(dx, dy, dc) for dx in range(4) for dy in range(4) for dc in range(2)],
        key=lambda t: -(ring(t[0], 4) + ring(t[1], 4) + 0.5 * t[2]),
    )
    bases = []
    for dx, dy, dc in places:
        x_there, y_there, c_there = lax.rem(x + dx, 4), lax.rem(y + dy, 4), lax.rem(core + dc, 2)
        bases.append((lax.rem(y_there, 2) * 16 + c_there, x_there * 2 + y_there // 2))

    def to_others(send):
        def step(i, carry):
            steps = jnp.where(lax.rem(i, 2) == 0, 4 + i // 2, 4 - (i + 1) // 2)
            z_there = lax.rem(z + steps, 8)
            for base_x, base_y in bases:
                send(base_x + 2 * z_there, base_y)
            return carry

        lax.fori_loop(0, 7, step, 0)
        for base_x, base_y in bases[:-1]:
            send(base_x + 2 * z, base_y)

    def row_of(device):
        return lax.rem(device, GY)

    entry = pltpu.get_barrier_semaphore()
    for i in range(1, GY):
        pl.semaphore_signal(entry, inc=1, device_id=(gx, row_of(gy + i)), device_id_type=MESH)

    def along_gx(sem):
        def step(i, carry):
            there = lax.rem(gx + i, GX)
            pl.semaphore_signal(sem, inc=1, device_id=(there, gy), device_id_type=MESH)
            return carry

        lax.fori_loop(1, GX, step, 0)

    along_gx(entry)

    for layer in range(2):
        static[layer] = occupancy[layer].astype(F32)
        static[2 + layer] = barrier[layer]
        static[4 + layer] = colour[layer].astype(F32)
        for section in range(SECTIONS):
            static[6 + 2 * section + layer] = direction[section, layer].astype(F32)
    for there in range(GY):
        rows = slice(4 * there, 4 * there + 4)
        fraction_sent[there] = jnp.concatenate([static[0, rows], static[1, rows]], 0)
    normal[...] = jnp.zeros_like(normal)
    shear[...] = jnp.zeros_like(shear)

    pl.semaphore_wait(entry, GX - 1 + GY - 1)
    along_gx(gather_sem)

    def gy_copy(i, source, target, send, recv):
        there = row_of(gy + i)
        return pltpu.make_async_remote_copy(
            source.at[there], target.at[gy], send, recv, device_id=(gx, there), device_id_type=MESH
        )

    for i in range(1, GY):
        gy_copy(i, fraction_sent, fraction_got, fraction_send, fraction_recv).start()
    fraction_got[gy] = fraction_sent[gy]
    green_tables(me, green)

    def wait_rows(source, target, send, recv, rows):
        copy = pltpu.make_async_remote_copy(
            source.at[pl.ds(0, rows)],
            target.at[pl.ds(0, rows)],
            send,
            recv,
            device_id=(gx + 1 - 2 * core, gy),
            device_id_type=MESH,
        )
        copy.wait_send()
        copy.wait_recv()

    wait_rows(fraction_sent, fraction_got, fraction_send, fraction_recv, GY - 1)
    upper = lax.broadcasted_iota(jnp.int32, (8, POINTS), 0) < 4
    pencil = jnp.concatenate([fraction_got[g] for g in range(GY)], 1)
    other = pltpu.roll(pencil, 4, 0)
    fraction_pencil[0] = jnp.where(upper, pencil, other)
    fraction_pencil[1] = jnp.where(upper, other, pencil)
    pl.semaphore_wait(gather_sem, GX - 1)

    def exchange(slot, rows):
        packed[slot, :, 0, :] = rows

        def send(there_x, there_y):
            pltpu.make_async_remote_copy(
                packed.at[slot, there_x * GY + there_y],
                landed.at[slot, me],
                send_sem.at[slot],
                recv_sem.at[slot],
                device_id=(there_x, there_y),
                device_id_type=MESH,
            ).start()

        to_others(send)
        landed[slot, me] = packed[slot, me]
        wait_rows(
            packed.at[slot], landed.at[slot], send_sem.at[slot], recv_sem.at[slot], DEVICES - 1
        )
        return landed[slot, :, 0, :]

    def sweep(i, carry):
        stress = []
        for p in range(2):
            stress_normal, stress_shear, _ = local_stress(normal[p], shear[p], fraction_pencil[p])
            stress.append(jnp.concatenate([stress_normal, stress_shear], 0))
        arrived = exchange(2 * i, forward_y(stress, dft, turn_y))
        arrived = exchange(
            2 * i + 1, spectral(arrived, dft, turn_x, forward4, inverse4, green)
        )
        change = inverse_y(arrived, dft, turn_y)
        for p in range(2):
            normal[p] += change[p][:8]
            shear[p] += change[p][8:]
        return carry

    up, down = lax.rem(gx + 1, GX), lax.rem(gx + GX - 1, GX)
    after, before = row_of(gy + 1), row_of(gy + GY - 1)
    first, last = pl.ds(0, 8), pl.ds(ROWS - 8, 8)
    halos = [
        (static, static_y.at[0], (gx, before)),
        (static, static_y.at[1], (gx, after)),
        (static.at[:, first], static_x.at[0], (down, gy)),
        (static.at[:, last], static_x.at[1], (up, gy)),
        (static.at[:, first], static_corner.at[0], (down, before)),
        (static.at[:, first], static_corner.at[1], (down, after)),
        (static.at[:, last], static_corner.at[2], (up, before)),
        (static.at[:, last], static_corner.at[3], (up, after)),
    ]
    halos = [
        pltpu.make_async_remote_copy(
            source, target, static_send.at[k], static_recv.at[k], device_id=there, device_id_type=MESH
        )
        for k, (source, target, there) in enumerate(halos)
    ]
    for copy in halos:
        copy.start()

    lax.fori_loop(0, ITERS, sweep, 0)

    energies = []
    for p in range(2):
        stress_normal, stress_shear, excess = local_stress(normal[p], shear[p], fraction_pencil[p])
        density = stress_normal * excess + 2.0 * stress_shear * shear[p]
        energies.append(0.5 * (density + pltpu.roll(density, 4, 0)))
    energy = jnp.where(upper, energies[0], energies[1])
    shears = jnp.where(upper, shear[0], pltpu.roll(shear[1], 4, 0))
    left = lax.broadcasted_iota(jnp.int32, (8, COLS), 1) < COLS // 2

    def block(values, g):
        return values[:, COLS * (g % GY) : COLS * (g % GY) + COLS]

    for g in range(GY):
        strain_sent[g, 0:8] = block(normal[0], g)
        strain_sent[g, 8:16] = block(normal[1], g)
        strain_sent[g, 16:24] = block(shears, g)
        energy_sent[g, :, :COLS] = block(energy, g)
        energy_sent[g, :, COLS:] = jnp.where(left, block(energy, g + 1), block(energy, g - 1))
    for i in range(1, GY):
        gy_copy(i, energy_sent, energy_got, last_send.at[0], last_recv.at[0]).start()
    for i in range(1, GY):
        gy_copy(i, strain_sent, strain_got, last_send.at[1], last_recv.at[1]).start()

    def edge_copy(g, slot, there):
        return pltpu.make_async_remote_copy(
            energy_sent.at[g],
            energy_got.at[GY + slot],
            edge_send.at[slot],
            edge_recv.at[slot],
            device_id=(there, g),
            device_id_type=MESH,
        )

    @pl.when(gy == 0)
    def _():
        for g in range(GY):
            edge_copy(g, 0, down).start()

    @pl.when(gy == GY - 1)
    def _():
        for g in range(GY):
            edge_copy(g, 1, up).start()

    energy_got[gy] = energy_sent[gy]
    strain_got[gy] = strain_sent[gy]

    for copy in halos:
        copy.wait()
    narrow = lax.broadcasted_iota(jnp.int32, (8, COLS), 0) < 4
    left_block = lax.broadcasted_iota(jnp.int32, (ROWS, COLS), 1) < COLS // 2

    def extended(k):
        side = jnp.where(left_block, static_y[0, k], static_y[1, k])
        edge = jnp.where(narrow, static_x[0, k], static_x[1, k])
        after_edge = jnp.where(narrow, static_corner[0, k], static_corner[2, k])
        before_edge = jnp.where(narrow, static_corner[1, k], static_corner[3, k])
        corner = jnp.where(left, after_edge, before_edge)
        return jnp.concatenate(
            [
                jnp.concatenate([static[k], side], 1),
                jnp.concatenate([edge, corner], 1),
            ],
            0,
        )

    fields = [extended(k) for k in range(STATIC)]

    wait_rows(energy_sent, energy_got, last_send.at[0], last_recv.at[0], GY - 1)
    for slot in range(2):
        edge_copy(0, slot, up).wait_recv()
    low = lax.broadcasted_iota(jnp.int32, (8, 2 * COLS), 0) < 4

    for layer in range(2):
        pieces = []
        for pair in range(GY // 2 + 1):
            one, two = energy_got[2 * pair], energy_got[2 * pair + 1]
            if layer == 0:
                pieces.append(jnp.where(low, one, pltpu.roll(two, 4, 0)))
            else:
                pieces.append(jnp.where(low, pltpu.roll(one, 4, 0), two))
        drive = fields[2 + layer] + elastic_weight * jnp.concatenate(pieces, 0) + base_rate
        sites = fields[layer]
        tall, wide = ROWS + 8, 2 * COLS
        for section in range(SECTIONS):
            way = fields[6 + 2 * section + layer]
            above, below = pltpu.roll(sites, 1, 0), pltpu.roll(sites, tall - 1, 0)
            ahead, behind = pltpu.roll(sites, wide - 1, 1), pltpu.roll(sites, 1, 1)
            neighbours = above + below + behind + ahead
            rate = 1.0 / (1.0 + jnp.exp(bond_energy * neighbours - drive))
            target = jnp.where(
                way == 0.0,
                below,
                jnp.where(way == 1.0, above, jnp.where(way == 2.0, ahead, behind)),
            )
            flux = jnp.where(
                fields[4 + layer] == float(section), rate * sites * (1.0 - target), 0.0
            )
            parted = [jnp.where(way == float(number), flux, 0.0) for number in range(4)]
            sites = (
                sites
                - flux
                + (
                    pltpu.roll(parted[0], 1, 0)
                    + pltpu.roll(parted[1], tall - 1, 0)
                    + pltpu.roll(parted[2], 1, 1)
                    + pltpu.roll(parted[3], wide - 1, 1)
                )
            )
        composition_out[layer] = sites[:ROWS, :COLS]

    wait_rows(strain_sent, strain_got, last_send.at[1], last_recv.at[1], GY - 1)
    for g in range(GY):
        rows = slice(4 * g, 4 * g + 4)
        for layer in range(2):
            strain_out[0, layer, rows] = strain_got[g, 8 * layer : 8 * layer + 4]
            strain_out[1, layer, rows] = strain_got[g, 8 * layer + 4 : 8 * layer + 8]
            strain_out[2, layer, rows] = strain_got[g, 16 + 4 * layer : 20 + 4 * layer]

    @pl.when(gy == 0)
    def _():
        for g in range(GY):
            edge_copy(g, 0, down).wait_send()

    @pl.when(gy == GY - 1)
    def _():
        for g in range(GY):
            edge_copy(g, 1, up).wait_send()


def on_device(occupancy, colour, hop_direction, barrier):
    operands = (occupancy, colour, hop_direction, barrier) + tuple(
        jnp.asarray(table) for table in tables()
    )
    vmem = pl.BlockSpec(memory_space=pltpu.VMEM)
    dma = pltpu.SemaphoreType.DMA
    return pl.pallas_call(
        kernel,
        out_shape=(
            jax.ShapeDtypeStruct((3, 2, ROWS, COLS), F32),
            jax.ShapeDtypeStruct((2, ROWS, COLS), F32),
        ),
        in_specs=[vmem] * len(operands),
        out_specs=(vmem, vmem),
        scratch_shapes=[
            pltpu.VMEM((3, 256, 128), F32),
            pltpu.VMEM((2, 8, POINTS), F32),
            pltpu.VMEM((2, 8, POINTS), F32),
            pltpu.VMEM((2, 8, POINTS), F32),
            pltpu.VMEM((2 * ITERS, DEVICES, 1, 128), F32),
            pltpu.VMEM((2 * ITERS, DEVICES, 1, 128), F32),
            pltpu.VMEM((GY, 8, COLS), F32),
            pltpu.VMEM((GY, 8, COLS), F32),
            pltpu.VMEM((STATIC, ROWS, COLS), F32),
            pltpu.VMEM((2, STATIC, ROWS, COLS), F32),
            pltpu.VMEM((2, STATIC, 8, COLS), F32),
            pltpu.VMEM((4, STATIC, 8, COLS), F32),
            pltpu.VMEM((GY, 24, COLS), F32),
            pltpu.VMEM((GY, 24, COLS), F32),
            pltpu.VMEM((GY, 8, 2 * COLS), F32),
            pltpu.VMEM((GY + 2, 8, 2 * COLS), F32),
            pltpu.SemaphoreType.REGULAR,
            dma((2 * ITERS,)),
            dma((2 * ITERS,)),
            dma,
            dma,
            dma((8,)),
            dma((8,)),
            dma((2,)),
            dma((2,)),
            dma((2,)),
            dma((2,)),
        ],
        compiler_params=pltpu.CompilerParams(
            collective_id=0, has_side_effects=True, vmem_limit_bytes=40 * 1024 * 1024
        ),
        name="film",
    )(*operands)


def solution(mesh):
    placed = (
        P(None, "gx", "gy"),
        P(None, "gx", "gy"),
        P(None, None, "gx", "gy"),
        P(None, "gx", "gy"),
    )
    return jax.shard_map(
        on_device,
        mesh=mesh,
        in_specs=placed,
        out_specs=(P(None, None, "gx", "gy"), P(None, "gx", "gy")),
        check_vma=False,
    )
```

```python
import math

import jax
import jax.numpy as jnp
import ml_dtypes
import numpy as np
from jax import lax
from jax.experimental import pallas as pl
from jax.experimental.pallas import tpu as pltpu
from jax.sharding import PartitionSpec as P

MESH = pl.DeviceIdType.MESH
F32 = jnp.float32
BF16 = jnp.bfloat16

ITERS = 3
SECTIONS = 2
GX, GY = 32, 8
DEVICES = GX * GY
POINTS = 1024
ROWS, COLS = POINTS // GX, POINTS // GY
STATIC = 10

lame_silicon = 1.2
lame_germanium = 0.9
shear_silicon = 1.0
shear_germanium = 0.8
lame_medium = 1.05
shear_medium = 0.9
elastic_weight = 2.0
bond_energy = 0.7
base_rate = 1.0


def split(values):
    high = values.astype(ml_dtypes.bfloat16)
    return high, (values - high.astype(np.float64)).astype(ml_dtypes.bfloat16)


def waves(angle, axis):
    return np.concatenate([np.cos(angle), np.sin(angle)], axis)


def tables():
    index = np.arange(256)
    angle = 2 * np.pi * (np.outer(index, index) % 256) / 256
    coarse = 2 * np.pi * (np.outer(index, index // 8) % 32) / 32
    dft = split(waves(angle, 1)) + split(waves(coarse, 1))
    lane = np.arange(128)
    turn_x = waves(2 * np.pi * np.outer(index, lane % 4) / POINTS, 0)
    turn_first = waves(2 * np.pi * np.outer(index, lane // 16 * 4 + lane % 4) / POINTS, 0)
    turn_y = waves(2 * np.pi * np.outer(np.arange(64) // 16, index) / POINTS, 0).reshape(2, 64, 256)
    stress = -2.0 * (lame_germanium + shear_germanium)
    angle = 2 * np.pi * np.outer(np.arange(16) // 4, np.arange(POINTS)) / POINTS
    turn_own = stress * np.stack([np.cos(angle), np.sin(angle)])
    turn_own = turn_own.reshape(2, 16, GY, COLS).transpose(2, 0, 1, 3)
    part, freq, comp, quad = lane // 64, lane // 16 % 4, lane // 4 % 4, lane % 4
    turns = np.outer(quad, quad) % 4
    cos4, sin4 = np.array([1, 0, -1, 0])[turns], np.array([0, 1, 0, -1])[turns]
    same_freq = freq[:, None] == freq[None, :]
    same_part = part[:, None] == part[None, :]
    to_real = part[None, :] == 0
    used = (comp[None, :] < 3) & same_freq
    forward = np.where(same_part, cos4, np.where(to_real, sin4, -sin4))
    forward4 = np.concatenate([forward * (used & (comp[:, None] == c)) for c in range(3)], 1)
    inverse = np.where(same_part, cos4, np.where(to_real, -sin4, sin4))
    inverse = inverse * (used & (comp[:, None] == comp[None, :]))
    turned = np.concatenate([-inverse[:, 64:], inverse[:, :64]], 1)
    inverse4 = np.concatenate([inverse, turned], 1)
    first4 = np.where((comp == 0)[:, None], forward4[:, :128], 0)
    picked = np.zeros((256, 128))
    for p in range(2):
        for n in range(128):
            picked[p * 128 + n] = first4[p * 64 + n // 4 % 4 * 16 + n % 4]
    small = np.concatenate([forward4, inverse4, picked[:128], picked[128:]], 1)
    return (
        np.concatenate(dft, 0),
        small.astype(ml_dtypes.bfloat16),
        np.concatenate([turn_x, turn_first], 0).reshape(4, 256, 128).astype(np.float32),
        turn_y.astype(np.float32),
        turn_own.astype(np.float32),
    )


def halves(values):
    high = values.astype(BF16)
    return high, (values - high.astype(F32)).astype(BF16)


def dot(left, right, dims):
    return lax.dot_general(left, right, (dims, ((), ())), preferred_element_type=F32)


def table_left(dft, values):
    high, low = halves(values)
    wide = dot(dft[0][...], jnp.concatenate([high, low], 1), ((1,), (0,)))
    return wide[:, :128] + wide[:, 128:] + dot(dft[1][...], high, ((1,), (0,)))


def table_left_turned(dft, rows):
    high, low = halves(rows)
    wide = dot(dft[0][...], jnp.concatenate([high, low], 0), ((1,), (1,)))
    return wide[:, :128] + wide[:, 128:] + dot(dft[1][...], high, ((1,), (1,)))


def three(left, right, dims):
    return dot(left[0], right[0], dims) + dot(left[0], right[1], dims) + dot(left[1], right[0], dims)


def exact(values, table):
    return dot(jnp.concatenate(halves(values), 1), jnp.concatenate([table, table], 0), ((1,), (0,)))


def green_tables(device, green):
    shape = (256, 128)
    lane = lax.broadcasted_iota(jnp.int32, shape, 1)
    comp = lax.rem(lane // 4, 4)
    index_x = lax.broadcasted_iota(jnp.int32, shape, 0) + 256 * lax.rem(lane, 4)
    index_y = 4 * device + lax.rem(lane // 16, 4)
    unit = 2.0 * math.pi / POINTS
    a = jnp.where(index_x < POINTS // 2, index_x, index_x - POINTS).astype(F32) * unit
    b = jnp.where(index_y < POINTS // 2, index_y, index_y - POINTS).astype(F32) * unit
    ratio = (lame_medium + shear_medium) / (lame_medium + 2.0 * shear_medium)
    squared = a * a + b * b
    positive = squared > 0
    inverse_sq = jnp.where(positive, 1.0 / jnp.where(positive, squared, 1.0), 0.0)
    base = inverse_sq * (-1.0 / (shear_medium * POINTS * POINTS))
    edge_x = (index_x == POINTS // 2).astype(F32)
    edge_y = (index_y == POINTS // 2).astype(F32)
    odd = base * (1.0 - jnp.abs(edge_x - edge_y))
    aa, bb, ab = a * a, b * b, a * b
    xx_xx = (aa - ratio * aa * aa * inverse_sq) * base
    yy_yy = (bb - ratio * bb * bb * inverse_sq) * base
    xx_yy = -ratio * aa * bb * inverse_sq * base
    xx_xy = (ab - 2.0 * ratio * aa * ab * inverse_sq) * odd
    yy_xy = (ab - 2.0 * ratio * bb * ab * inverse_sq) * odd
    xy_xy = 0.5 * (aa + bb - 4.0 * ratio * aa * bb * inverse_sq) * base

    def pick(first, second, third):
        return jnp.where(
            comp == 0, first, jnp.where(comp == 1, second, jnp.where(comp == 2, third, 0.0))
        )

    green[0] = pick(xx_xx, xx_yy, 0.5 * xx_xy)
    green[1] = pick(xx_yy, yy_yy, 0.5 * yy_xy)
    green[2] = pick(xx_xy, yy_xy, xy_xy)


def crossing(shape):
    return jnp.where(lax.broadcasted_iota(jnp.int32, shape, 1) < 64, 1.0, -1.0)


def spectral(received, dft, turn, small, green):
    sign = crossing((256, 128))
    swapped = pltpu.roll(received, 64, 1) * sign
    first = table_left(dft, jnp.concatenate([received, swapped], 0))
    turned = turn[0] * first + turn[1] * (pltpu.roll(first, 64, 1) * sign)
    spread = exact(turned, small[:, :384])
    mapped = (
        green[0] * spread[:, :128] + green[1] * spread[:, 128:256] + green[2] * spread[:, 256:]
    )
    return spectral_back(mapped, dft, turn, small)


def spectral_back(mapped, dft, turn, small):
    back = exact(mapped, small[:, 384:640])
    plain, crossed = back[:, :128], back[:, 128:]
    values = turn[0] * plain + turn[1] * crossed
    crossed = turn[0] * crossed - turn[1] * plain
    return table_left(dft, jnp.concatenate([values, crossed], 0))


def spectral_first(received, dft, coarse, turn, small, green):
    real, imag = received[:, :128], received[:, 128:]
    both = jnp.concatenate(
        [jnp.concatenate([real, imag], 1), jnp.concatenate([imag, -real], 1)], 0
    )
    first = three([part[...] for part in coarse], halves(both), ((1,), (0,)))
    real, imag = first[:, :128], first[:, 128:]
    real, imag = turn[2] * real + turn[3] * imag, turn[2] * imag - turn[3] * real
    spread = exact(
        jnp.concatenate([real, imag], 1),
        jnp.concatenate([small[:, 640:768], small[:, 768:896]], 0),
    )
    return spectral_back((green[0] + green[1]) * spread, dft, turn, small)


def first_y(fields, dft, turn, odd):
    upper = lax.broadcasted_iota(jnp.int32, (8, COLS), 0) < 4
    spread = []
    for field in fields:
        pieces = []
        for t in range(ROWS // 8):
            tile = field[8 * t : 8 * t + 8]
            other = pltpu.roll(tile, 4, 0)
            one, two = jnp.where(upper, tile, other), jnp.where(upper, other, tile)
            pieces += [one, one, two, two]
        spread.append(jnp.concatenate(pieces, 0))
    real, imag = spread
    cos, sin = (jnp.concatenate([turn[k]] * 8, 0) for k in range(2))
    real, imag = cos * real + sin * imag, cos * imag - sin * real
    rows = jnp.concatenate(
        [jnp.concatenate([real, imag], 1), jnp.concatenate([imag, -real], 1)], 0
    )
    table = [jnp.concatenate([part[:, :128], part[:, 256:384]], 1) for part in dft]
    out = three(table, halves(rows), ((1,), (1,)))
    flip = lax.rem(lax.broadcasted_iota(jnp.int32, out.shape, 0), 2) * odd
    return out * (1 - 2 * flip).astype(F32)


def four(parts, sign):
    (r0, r1, r2, r3), (i0, i1, i2, i3) = parts
    er, ei, dr, di = r0 + r2, i0 + i2, r0 - r2, i0 - i2
    fr, fi, gr, gi = r1 + r3, i1 + i3, r1 - r3, i1 - i3
    up_r, up_i = dr - gi, di + gr
    down_r, down_i = dr + gi, di - gr
    if sign < 0:
        up_r, up_i, down_r, down_i = down_r, down_i, up_r, up_i
    return (er + fr, up_r, er - fr, down_r), (ei + fi, up_i, ei - fi, down_i)


def forward_y(stress, dft, turn_y):
    parts = [[field[:, 256 * a : 256 * a + 256] for a in range(4)] for field in stress]
    real, imag = (jnp.concatenate(list(part), 0) for part in four(parts, -1))
    turned_real = turn_y[0] * real + turn_y[1] * imag
    turned_imag = turn_y[0] * imag - turn_y[1] * real
    rows = jnp.concatenate(
        [
            jnp.concatenate([turned_real, turned_imag], 1),
            jnp.concatenate([turned_imag, -turned_real], 1),
        ],
        0,
    )
    return table_left_turned(dft, rows)


def inverse_y(received, dft, turn_y):
    across = received.T
    real, imag = across[:64], across[64:]
    rows = jnp.concatenate(
        [jnp.concatenate([real, -imag], 1), jnp.concatenate([imag, real], 1)], 0
    )
    both = three(halves(rows), [part[...] for part in dft], ((1,), (1,)))
    real, imag = both[:64], both[64:]
    turned_real = turn_y[0] * real - turn_y[1] * imag
    turned_imag = turn_y[0] * imag + turn_y[1] * real
    parts = [
        [part[16 * j : 16 * j + 16] for j in range(4)] for part in (turned_real, turned_imag)
    ]
    return [jnp.concatenate(list(part), 1) for part in four(parts, 1)]


def local_stress(normal, shear, fraction):
    lame_field = lame_silicon + (lame_germanium - lame_silicon) * fraction
    shear_field = 2.0 * (shear_silicon + (shear_germanium - shear_silicon) * fraction)
    excess = normal - fraction
    trace = excess + pltpu.roll(excess, 4, 0)
    return lame_field * trace + shear_field * excess, shear_field * shear, excess


def ring(steps, size):
    return min(steps % size, -steps % size)


def kernel(
    occupancy_in,
    colour_in,
    direction_in,
    barrier_in,
    dft_in,
    small_in,
    turn_in,
    turn_y_in,
    turn_own_in,
    strain_out,
    composition_out,
    occupancy,
    colour,
    direction,
    barrier,
    dfts,
    small,
    turn,
    turn_y,
    turn_own,
    green,
    normal,
    shear,
    fraction_pencil,
    first_sent,
    first_got,
    packed,
    landed,
    fraction_sent,
    fraction_got,
    static,
    rows_sent,
    rows_got,
    cols_sent,
    cols_got,
    corner_got,
    fields,
    strain_sent,
    strain_got,
    energy_sent,
    energy_got,
    input_sem,
    first_sem,
    send_sem,
    recv_sem,
    fraction_sem,
    halo_send,
    halo_recv,
    last_send,
    last_recv,
    edge_send,
    edge_recv,
):
    gx, gy = lax.axis_index("gx"), lax.axis_index("gy")
    me = gx * GY + gy
    z, core = lax.rem(gx // 2, 8), lax.rem(gx, 2)
    x, y = gy // 2, lax.rem(gy, 2) * 2 + gx // 16

    inputs = [
        (occupancy_in, occupancy),
        (dft_in, dfts),
        (turn_own_in.at[gy], turn_own),
        (barrier_in, barrier),
        (colour_in, colour),
        (direction_in, direction),
        (small_in, small),
        (turn_in, turn),
        (turn_y_in, turn_y),
    ]
    inputs = [
        pltpu.make_async_copy(source, target, input_sem.at[k])
        for k, (source, target) in enumerate(inputs)
    ]
    for copy in inputs:
        copy.start()

    places = sorted(
        [(dx, dy, dc) for dx in range(4) for dy in range(4) for dc in range(2)],
        key=lambda t: -(ring(t[0], 4) + ring(t[1], 4) + 0.5 * t[2]),
    )
    bases = []
    for dx, dy, dc in places:
        x_there, y_there, c_there = lax.rem(x + dx, 4), lax.rem(y + dy, 4), lax.rem(core + dc, 2)
        bases.append((lax.rem(y_there, 2) * 16 + c_there, x_there * 2 + y_there // 2))

    def to_others(send):
        def step(i, carry):
            steps = jnp.where(lax.rem(i, 2) == 0, 4 + i // 2, 4 - (i + 1) // 2)
            z_there = lax.rem(z + steps, 8)
            for base_x, base_y in bases:
                send(base_x + 2 * z_there, base_y)
            return carry

        lax.fori_loop(0, 7, step, 0)
        for base_x, base_y in bases[:-1]:
            send(base_x + 2 * z, base_y)

    entry = pltpu.get_barrier_semaphore()
    to_others(
        lambda there_x, there_y: pl.semaphore_signal(
            entry, inc=1, device_id=(there_x, there_y), device_id_type=MESH
        )
    )

    dft = (dfts.at[pl.ds(0, 256)], dfts.at[pl.ds(256, 256)])
    coarse = (dfts.at[pl.ds(512, 256)], dfts.at[pl.ds(768, 256)])

    for copy in inputs[:3]:
        copy.wait()
    for layer in range(2):
        static[layer] = occupancy[layer].astype(F32)
    rows = first_y([static[0], static[1]], dft, turn_own, lax.rem(gy, 2))
    first_sent[:, 0, :] = rows[:, :128]
    first_sent[:, 1, :] = rows[:, 128:]
    first_got[me] = first_sent[me]
    for there in range(GY):
        part = slice(4 * there, 4 * there + 4)
        fraction_sent[there] = jnp.concatenate([static[0, part], static[1, part]], 0)
    fraction_got[gy] = fraction_sent[gy]

    pl.semaphore_wait(entry, DEVICES - 1)

    def send_first(there_x, there_y):
        pltpu.make_async_remote_copy(
            first_sent.at[there_x * GY + there_y],
            first_got.at[me],
            first_sem.at[0],
            first_sem.at[1],
            device_id=(there_x, there_y),
            device_id_type=MESH,
        ).start()

    to_others(send_first)

    def total(source, target, send, recv, rows):
        return pltpu.make_async_remote_copy(
            source.at[pl.ds(0, rows)],
            target.at[pl.ds(0, rows)],
            send,
            recv,
            device_id=(gx + 1 - 2 * core, gy),
            device_id_type=MESH,
        )

    offsets = sorted(
        [(dx, dy) for dx in range(4) for dy in range(2) if dx + dy > 0],
        key=lambda t: -(ring(t[0], 4) + 2 * t[1]),
    )
    peers = [lax.rem(x + dx, 4) * 2 + lax.rem(gy + dy, 2) for dx, dy in offsets]

    def to_peers(source, target, send, recv):
        for there in peers:
            pltpu.make_async_remote_copy(
                source.at[there],
                target.at[gy],
                send,
                recv,
                device_id=(gx, there),
                device_id_type=MESH,
            ).start()
        return total(source, target, send, recv, GY - 1)

    fraction_copies = to_peers(fraction_sent, fraction_got, fraction_sem.at[0], fraction_sem.at[1])

    for copy in inputs[3:]:
        copy.wait()
    for layer in range(2):
        static[2 + layer] = barrier[layer]
        static[4 + layer] = colour[layer].astype(F32)
        for section in range(SECTIONS):
            static[6 + 2 * section + layer] = direction[section, layer].astype(F32)
    upper = lax.broadcasted_iota(jnp.int32, (8, COLS), 0) < 4
    for kind in range(STATIC // 2):
        one, two = static[2 * kind], static[2 * kind + 1]
        rows_sent[0, kind] = jnp.where(upper, one[:8], pltpu.roll(two[:8], 4, 0))
        rows_sent[1, kind] = jnp.where(upper, pltpu.roll(one[-8:], 4, 0), two[-8:])
    flat = [static[k] for k in range(STATIC)] + [jnp.zeros((64, COLS), F32)]
    across = jnp.concatenate(flat, 0).T
    cols_sent[0] = across[:8]
    cols_sent[1] = across[-8:]

    up, down = lax.rem(gx + 1, GX), lax.rem(gx + GX - 1, GX)
    after, before = lax.rem(gy + 1, GY), lax.rem(gy + GY - 1, GY)
    halos = [
        (rows_sent.at[0], rows_got.at[0], (down, gy)),
        (rows_sent.at[1], rows_got.at[1], (up, gy)),
        (cols_sent.at[0], cols_got.at[0], (gx, before)),
        (cols_sent.at[1], cols_got.at[1], (gx, after)),
        (cols_sent.at[0], corner_got.at[0], (down, before)),
        (cols_sent.at[1], corner_got.at[1], (down, after)),
        (cols_sent.at[0], corner_got.at[2], (up, before)),
        (cols_sent.at[1], corner_got.at[3], (up, after)),
    ]
    halos = [
        pltpu.make_async_remote_copy(
            source, target, halo_send.at[k], halo_recv.at[k], device_id=there, device_id_type=MESH
        )
        for k, (source, target, there) in enumerate(halos)
    ]
    for copy in halos:
        copy.start()
    green_tables(me, green)

    total(first_sent, first_got, first_sem.at[0], first_sem.at[1], DEVICES - 1).wait_recv()
    received = jnp.concatenate([first_got[:, 0, :], first_got[:, 1, :]], 1)

    def start_exchange(slot, rows):
        packed[slot, :, 0, :] = rows

        def send(there_x, there_y):
            pltpu.make_async_remote_copy(
                packed.at[slot, there_x * GY + there_y],
                landed.at[slot, me],
                send_sem.at[slot],
                recv_sem.at[slot],
                device_id=(there_x, there_y),
                device_id_type=MESH,
            ).start()

        to_others(send)
        landed[slot, me] = packed[slot, me]

    def exchanged(slot):
        return total(
            packed.at[slot], landed.at[slot], send_sem.at[slot], recv_sem.at[slot], DEVICES - 1
        )

    def end_exchange(slot):
        exchanged(slot).wait_recv()
        return landed[slot, :, 0, :]

    start_exchange(0, spectral_first(received, dft, coarse, turn, small, green))

    fraction_copies.wait_recv()
    pencil = jnp.concatenate([fraction_got[g] for g in range(GY)], 1)
    other = pltpu.roll(pencil, 4, 0)
    upper_wide = lax.broadcasted_iota(jnp.int32, (8, POINTS), 0) < 4
    fraction_pencil[0] = jnp.where(upper_wide, pencil, other)
    fraction_pencil[1] = jnp.where(upper_wide, other, pencil)
    for copy in halos:
        copy.wait_recv()

    def side(ahead, behind):
        gap = jnp.zeros((COLS - 16, 384), F32)
        return jnp.concatenate([ahead, gap, behind], 0).T

    beside = side(cols_got[0], cols_got[1])
    below = side(corner_got[0], corner_got[1])
    above = side(corner_got[2], corner_got[3])
    for k in range(STATIC):
        kind, layer = k // 2, k % 2
        part = slice(ROWS * k, ROWS * k + ROWS)
        fields[k, :ROWS, :COLS] = static[k]
        fields[k, :ROWS, COLS:] = beside[part]
        low, high = rows_got[0, kind], rows_got[1, kind]
        if layer == 0:
            high = pltpu.roll(high, 4, 0)
        else:
            low = pltpu.roll(low, 4, 0)
        fields[k, ROWS:, :COLS] = jnp.where(upper, low, high)
        fields[k, ROWS:, COLS:] = jnp.where(upper, below[part][:8], above[part][-8:])

    change = inverse_y(end_exchange(0), dft, turn_y)
    for p in range(2):
        normal[p] = change[p][:8]
        shear[p] = change[p][8:]

    def sweep(i, carry):
        stress = []
        for p in range(2):
            stress_normal, stress_shear, _ = local_stress(normal[p], shear[p], fraction_pencil[p])
            stress.append(jnp.concatenate([stress_normal, stress_shear], 0))
        start_exchange(2 * i + 1, forward_y(stress, dft, turn_y))
        arrived = end_exchange(2 * i + 1)
        start_exchange(2 * i + 2, spectral(arrived, dft, turn, small, green))
        change = inverse_y(end_exchange(2 * i + 2), dft, turn_y)
        for p in range(2):
            normal[p] += change[p][:8]
            shear[p] += change[p][8:]
        return carry

    lax.fori_loop(0, ITERS - 1, sweep, 0)

    energies = []
    for p in range(2):
        stress_normal, stress_shear, excess = local_stress(normal[p], shear[p], fraction_pencil[p])
        density = stress_normal * excess + 2.0 * stress_shear * shear[p]
        energies.append(0.5 * (density + pltpu.roll(density, 4, 0)))
    energy = jnp.where(upper_wide, energies[0], energies[1])
    shears = jnp.where(upper_wide, shear[0], pltpu.roll(shear[1], 4, 0))
    left = lax.broadcasted_iota(jnp.int32, (8, COLS), 1) < COLS // 2

    def block(values, g):
        return values[:, COLS * (g % GY) : COLS * (g % GY) + COLS]

    for g in range(GY):
        energy_sent[g, :, :COLS] = block(energy, g)
        energy_sent[g, :, COLS:] = jnp.where(left, block(energy, g + 1), block(energy, g - 1))

    def edge_copy(g, slot, there):
        return pltpu.make_async_remote_copy(
            energy_sent.at[g],
            energy_got.at[GY + slot],
            edge_send.at[slot],
            edge_recv.at[slot],
            device_id=(there, g),
            device_id_type=MESH,
        )

    @pl.when(gy == 0)
    def _():
        for g in range(GY):
            edge_copy(g, 0, down).start()

    @pl.when(gy == GY - 1)
    def _():
        for g in range(GY):
            edge_copy(g, 1, up).start()

    energy_copies = to_peers(energy_sent, energy_got, last_send.at[0], last_recv.at[0])
    for g in range(GY):
        strain_sent[g, 0:8] = block(normal[0], g)
        strain_sent[g, 8:16] = block(normal[1], g)
        strain_sent[g, 16:24] = block(shears, g)
    strain_copies = to_peers(strain_sent, strain_got, last_send.at[1], last_recv.at[1])
    energy_got[gy] = energy_sent[gy]
    strain_got[gy] = strain_sent[gy]

    total(first_sent, first_got, first_sem.at[0], first_sem.at[1], DEVICES - 1).wait_send()
    fraction_copies.wait_send()
    for copy in halos:
        copy.wait_send()
    for slot in range(2 * ITERS - 1):
        exchanged(slot).wait_send()

    energy_copies.wait_recv()
    for slot in range(2):
        edge_copy(0, slot, up).wait_recv()
    low = lax.broadcasted_iota(jnp.int32, (8, 2 * COLS), 0) < 4

    for layer in range(2):
        pieces = []
        for pair in range(GY // 2 + 1):
            one, two = energy_got[2 * pair], energy_got[2 * pair + 1]
            if layer == 0:
                pieces.append(jnp.where(low, one, pltpu.roll(two, 4, 0)))
            else:
                pieces.append(jnp.where(low, pltpu.roll(one, 4, 0), two))
        drive = fields[2 + layer] + elastic_weight * jnp.concatenate(pieces, 0) + base_rate
        sites = fields[layer]
        tall, wide = ROWS + 8, 2 * COLS
        for section in range(SECTIONS):
            way = fields[6 + 2 * section + layer]
            above, below = pltpu.roll(sites, 1, 0), pltpu.roll(sites, tall - 1, 0)
            ahead, behind = pltpu.roll(sites, wide - 1, 1), pltpu.roll(sites, 1, 1)
            neighbours = above + below + behind + ahead
            rate = 1.0 / (1.0 + jnp.exp(bond_energy * neighbours - drive))
            target = jnp.where(
                way == 0.0,
                below,
                jnp.where(way == 1.0, above, jnp.where(way == 2.0, ahead, behind)),
            )
            flux = jnp.where(
                fields[4 + layer] == float(section), rate * sites * (1.0 - target), 0.0
            )
            parted = [jnp.where(way == float(number), flux, 0.0) for number in range(4)]
            sites = (
                sites
                - flux
                + (
                    pltpu.roll(parted[0], 1, 0)
                    + pltpu.roll(parted[1], tall - 1, 0)
                    + pltpu.roll(parted[2], 1, 1)
                    + pltpu.roll(parted[3], wide - 1, 1)
                )
            )
        composition_out[layer] = sites[:ROWS, :COLS]

    strain_copies.wait_recv()
    for g in range(GY):
        rows = slice(4 * g, 4 * g + 4)
        for layer in range(2):
            strain_out[0, layer, rows] = strain_got[g, 8 * layer : 8 * layer + 4]
            strain_out[1, layer, rows] = strain_got[g, 8 * layer + 4 : 8 * layer + 8]
            strain_out[2, layer, rows] = strain_got[g, 16 + 4 * layer : 20 + 4 * layer]

    energy_copies.wait_send()
    strain_copies.wait_send()

    @pl.when(gy == 0)
    def _():
        for g in range(GY):
            edge_copy(g, 0, down).wait_send()

    @pl.when(gy == GY - 1)
    def _():
        for g in range(GY):
            edge_copy(g, 1, up).wait_send()


def on_device(occupancy, colour, hop_direction, barrier):
    operands = (occupancy, colour, hop_direction, barrier) + tuple(
        jnp.asarray(table) for table in tables()
    )
    vmem = pl.BlockSpec(memory_space=pltpu.VMEM)
    dma = pltpu.SemaphoreType.DMA
    exchanges = 2 * ITERS - 1
    return pl.pallas_call(
        kernel,
        out_shape=(
            jax.ShapeDtypeStruct((3, 2, ROWS, COLS), F32),
            jax.ShapeDtypeStruct((2, ROWS, COLS), F32),
        ),
        in_specs=[pl.BlockSpec(memory_space=pltpu.HBM)] * len(operands),
        out_specs=(vmem, vmem),
        scratch_shapes=[
            pltpu.VMEM((2, ROWS, COLS), jnp.int32),
            pltpu.VMEM((2, ROWS, COLS), jnp.int32),
            pltpu.VMEM((2, 2, ROWS, COLS), jnp.int32),
            pltpu.VMEM((2, ROWS, COLS), F32),
            pltpu.VMEM((1024, 512), BF16),
            pltpu.VMEM((128, 896), BF16),
            pltpu.VMEM((4, 256, 128), F32),
            pltpu.VMEM((2, 64, 256), F32),
            pltpu.VMEM((2, 16, COLS), F32),
            pltpu.VMEM((3, 256, 128), F32),
            pltpu.VMEM((2, 8, POINTS), F32),
            pltpu.VMEM((2, 8, POINTS), F32),
            pltpu.VMEM((2, 8, POINTS), F32),
            pltpu.VMEM((DEVICES, 2, 128), F32),
            pltpu.VMEM((DEVICES, 2, 128), F32),
            pltpu.VMEM((exchanges, DEVICES, 1, 128), F32),
            pltpu.VMEM((exchanges, DEVICES, 1, 128), F32),
            pltpu.VMEM((GY, 8, COLS), F32),
            pltpu.VMEM((GY, 8, COLS), F32),
            pltpu.VMEM((STATIC, ROWS, COLS), F32),
            pltpu.VMEM((2, STATIC // 2, 8, COLS), F32),
            pltpu.VMEM((2, STATIC // 2, 8, COLS), F32),
            pltpu.VMEM((2, 8, 384), F32),
            pltpu.VMEM((2, 8, 384), F32),
            pltpu.VMEM((4, 8, 384), F32),
            pltpu.VMEM((STATIC, ROWS + 8, 2 * COLS), F32),
            pltpu.VMEM((GY, 24, COLS), F32),
            pltpu.VMEM((GY, 24, COLS), F32),
            pltpu.VMEM((GY, 8, 2 * COLS), F32),
            pltpu.VMEM((GY + 2, 8, 2 * COLS), F32),
            dma((9,)),
            dma((2,)),
            dma((exchanges,)),
            dma((exchanges,)),
            dma((2,)),
            dma((8,)),
            dma((8,)),
            dma((2,)),
            dma((2,)),
            dma((2,)),
            dma((2,)),
        ],
        compiler_params=pltpu.CompilerParams(
            collective_id=0, has_side_effects=True, vmem_limit_bytes=62 * 1024 * 1024
        ),
        name="film",
    )(*operands)


def solution(mesh):
    placed = (
        P(None, "gx", "gy"),
        P(None, "gx", "gy"),
        P(None, None, "gx", "gy"),
        P(None, "gx", "gy"),
    )
    return jax.shard_map(
        on_device,
        mesh=mesh,
        in_specs=placed,
        out_specs=(P(None, None, "gx", "gy"), P(None, "gx", "gy")),
        check_vma=False,
    )
```

```python
import math

import jax
import jax.numpy as jnp
import ml_dtypes
import numpy as np
from jax import lax
from jax.experimental import pallas as pl
from jax.experimental.pallas import tpu as pltpu
from jax.sharding import PartitionSpec as P

MESH = pl.DeviceIdType.MESH
F32 = jnp.float32
BF16 = jnp.bfloat16

ITERS = 3
SECTIONS = 2
GX, GY = 32, 8
DEVICES = GX * GY
POINTS = 1024
ROWS, COLS = POINTS // GX, POINTS // GY
STATIC = 10

lame_silicon = 1.2
lame_germanium = 0.9
shear_silicon = 1.0
shear_germanium = 0.8
lame_medium = 1.05
shear_medium = 0.9
elastic_weight = 2.0
bond_energy = 0.7
base_rate = 1.0


def split(values):
    high = values.astype(ml_dtypes.bfloat16)
    return high, (values - high.astype(np.float64)).astype(ml_dtypes.bfloat16)


def waves(angle, axis):
    return np.concatenate([np.cos(angle), np.sin(angle)], axis)


def half_waves(angle):
    return np.concatenate([np.cos(angle[:144]), np.sin(angle[:128])], 0)


def tables():
    index = np.arange(256)
    angle = 2 * np.pi * (np.outer(index, index) % 256) / 256
    coarse = 2 * np.pi * (np.outer(index, index // 8) % 32) / 32
    order = np.concatenate([index[:129], 384 - index[129:]])
    both = np.concatenate([np.cos(angle[order]), np.sin(angle[order])], 1)
    back = np.concatenate([np.cos(angle[:, :128]), np.sin(angle[:, :128])], 1)
    back[:, 128] = np.cos(angle[:, 128])
    dft = split(half_waves(angle)) + split(half_waves(coarse)) + split(back)
    lane = np.arange(128)
    turn_x = waves(2 * np.pi * np.outer(order, lane % 4) / POINTS, 0)
    turn_first = waves(2 * np.pi * np.outer(order, lane // 16 * 4 + lane % 4) / POINTS, 0)
    turn_y = waves(2 * np.pi * np.outer(np.arange(64) // 16, index) / POINTS, 0).reshape(2, 64, 256)
    stress = -2.0 * (lame_germanium + shear_germanium)
    angle = 2 * np.pi * np.outer(np.arange(16) // 4, np.arange(POINTS)) / POINTS
    turn_own = stress * np.stack([np.cos(angle), np.sin(angle)])
    turn_own = turn_own.reshape(2, 16, GY, COLS).transpose(2, 0, 1, 3)
    part, freq, comp, quad = lane // 64, lane // 16 % 4, lane // 4 % 4, lane % 4
    turns = np.outer(quad, quad) % 4
    cos4, sin4 = np.array([1, 0, -1, 0])[turns], np.array([0, 1, 0, -1])[turns]
    same_freq = freq[:, None] == freq[None, :]
    same_part = part[:, None] == part[None, :]
    to_real = part[None, :] == 0
    used = (comp[None, :] < 3) & same_freq
    forward = np.where(same_part, cos4, np.where(to_real, sin4, -sin4))
    forward4 = np.concatenate([forward * (used & (comp[:, None] == c)) for c in range(3)], 1)
    inverse = np.where(same_part, cos4, np.where(to_real, -sin4, sin4))
    inverse = inverse * (used & (comp[:, None] == comp[None, :]))
    turned = np.concatenate([-inverse[:, 64:], inverse[:, :64]], 1)
    inverse4 = np.concatenate([inverse, turned], 1)
    first4 = np.where((comp == 0)[:, None], forward4[:, :128], 0)
    picked = np.zeros((256, 128))
    for p in range(2):
        for n in range(128):
            picked[p * 128 + n] = first4[p * 64 + n // 4 % 4 * 16 + n % 4]
    both = np.concatenate(split(both), 0)
    small = np.concatenate([forward4, inverse4, picked[:128], picked[128:]], 1)
    return (
        np.concatenate(dft, 0),
        both,
        small.astype(ml_dtypes.bfloat16),
        np.concatenate([turn_x, turn_first], 0).reshape(4, 256, 128).astype(np.float32),
        turn_y.astype(np.float32),
        turn_own.astype(np.float32),
    )


def halves(values):
    high = values.astype(BF16)
    return high, (values - high.astype(F32)).astype(BF16)


def dot(left, right, dims):
    return lax.dot_general(left, right, (dims, ((), ())), preferred_element_type=F32)


def wide(table, values, dims):
    high, low = halves(values)
    both = dot(table[0][...], jnp.concatenate([high, low], 1 - dims[1][0]), dims)
    return both[:, :128] + both[:, 128:] + dot(table[1][...], high, dims)


def narrow(table, values, dims):
    return three([part[...] for part in table], halves(values), dims)


def parity(dft, multiply, plain, crossed, dims):
    even, odd = multiply(dft[0], plain, dims), multiply(dft[1], crossed, dims)
    minus = even[:128] - odd
    return jnp.concatenate(
        [even[:128] + odd, first_row(even[128:136], minus[:8]), minus[8:]], 0
    )


def first_row(special, others):
    return jnp.where(lax.broadcasted_iota(jnp.int32, others.shape, 0) == 0, special, others)


def folded(values):
    return values[:128] + values[128:], values[:128] - values[128:]


def three(left, right, dims):
    return dot(left[0], right[0], dims) + dot(left[0], right[1], dims) + dot(left[1], right[0], dims)


def exact(values, table):
    return dot(jnp.concatenate(halves(values), 1), jnp.concatenate([table, table], 0), ((1,), (0,)))


def green_tables(device, green):
    shape = (256, 128)
    lane = lax.broadcasted_iota(jnp.int32, shape, 1)
    comp = lax.rem(lane // 4, 4)
    row = lax.broadcasted_iota(jnp.int32, shape, 0)
    index_x = jnp.where(row > 128, 384 - row, row) + 256 * lax.rem(lane, 4)
    index_y = 4 * jnp.where(device > 128, 384 - device, device) + lax.rem(lane // 16, 4)
    unit = 2.0 * math.pi / POINTS
    a = jnp.where(index_x < POINTS // 2, index_x, index_x - POINTS).astype(F32) * unit
    b = jnp.where(index_y < POINTS // 2, index_y, index_y - POINTS).astype(F32) * unit
    ratio = (lame_medium + shear_medium) / (lame_medium + 2.0 * shear_medium)
    squared = a * a + b * b
    positive = squared > 0
    inverse_sq = jnp.where(positive, 1.0 / jnp.where(positive, squared, 1.0), 0.0)
    base = inverse_sq * (-1.0 / (shear_medium * POINTS * POINTS))
    edge_x = (index_x == POINTS // 2).astype(F32)
    edge_y = (index_y == POINTS // 2).astype(F32)
    odd = base * (1.0 - jnp.abs(edge_x - edge_y))
    aa, bb, ab = a * a, b * b, a * b
    xx_xx = (aa - ratio * aa * aa * inverse_sq) * base
    yy_yy = (bb - ratio * bb * bb * inverse_sq) * base
    xx_yy = -ratio * aa * bb * inverse_sq * base
    xx_xy = (ab - 2.0 * ratio * aa * ab * inverse_sq) * odd
    yy_xy = (ab - 2.0 * ratio * bb * ab * inverse_sq) * odd
    xy_xy = 0.5 * (aa + bb - 4.0 * ratio * aa * bb * inverse_sq) * base

    def pick(first, second, third):
        return jnp.where(
            comp == 0, first, jnp.where(comp == 1, second, jnp.where(comp == 2, third, 0.0))
        )

    green[0] = pick(xx_xx, xx_yy, 0.5 * xx_xy)
    green[1] = pick(xx_yy, yy_yy, 0.5 * yy_xy)
    green[2] = pick(xx_xy, yy_xy, xy_xy)


def crossing(shape):
    return jnp.where(lax.broadcasted_iota(jnp.int32, shape, 1) < 64, 1.0, -1.0)


def spectral(received, dft, back, turn, small, green):
    sign = crossing((256, 128))
    swapped = pltpu.roll(received, 64, 1) * sign
    first = wide(dft, jnp.concatenate([received, swapped], 0), ((1,), (0,)))
    turned = turn[0] * first + turn[1] * (pltpu.roll(first, 64, 1) * sign)
    spread = exact(turned, small[:, :384])
    mapped = (
        green[0] * spread[:, :128] + green[1] * spread[:, 128:256] + green[2] * spread[:, 256:]
    )
    return spectral_back(mapped, back, turn, small)


def spectral_back(mapped, back, turn, small):
    both = exact(mapped, small[:, 384:640])
    plain, crossed = both[:, :128], both[:, 128:]
    values = turn[0] * plain + turn[1] * crossed
    crossed = turn[0] * crossed - turn[1] * plain
    even, odd = folded(values)[0], folded(crossed)[1]
    even = [first_row(values[:8], even[:8]), even[8:]]
    odd = [first_row(values[128:136], odd[:8]), odd[8:]]
    return wide(back, jnp.concatenate(even + odd, 0), ((1,), (0,)))


def spectral_first(received, coarse, back, turn, small, green):
    real, imag = received[:, :128], received[:, 128:]
    first = parity(coarse, narrow, received, jnp.concatenate([imag, -real], 1), ((1,), (0,)))
    real, imag = first[:, :128], first[:, 128:]
    real, imag = turn[2] * real + turn[3] * imag, turn[2] * imag - turn[3] * real
    spread = exact(
        jnp.concatenate([real, imag], 1),
        jnp.concatenate([small[:, 640:768], small[:, 768:896]], 0),
    )
    return spectral_back((green[0] + green[1]) * spread, back, turn, small)


def first_y(fields, dft, turn, odd):
    upper = lax.broadcasted_iota(jnp.int32, (8, COLS), 0) < 4
    spread = []
    for field in fields:
        pieces = []
        for t in range(ROWS // 8):
            tile = field[8 * t : 8 * t + 8]
            other = pltpu.roll(tile, 4, 0)
            one, two = jnp.where(upper, tile, other), jnp.where(upper, other, tile)
            pieces += [one, one, two, two]
        spread.append(jnp.concatenate(pieces, 0))
    real, imag = spread
    cos, sin = (jnp.concatenate([turn[k]] * 8, 0) for k in range(2))
    real, imag = cos * real + sin * imag, cos * imag - sin * real
    plain, crossed = jnp.concatenate([real, imag], 0), jnp.concatenate([imag, -real], 0)
    table = [[part.at[:, pl.ds(0, 128)] for part in parts] for parts in dft]
    out = parity(table, narrow, plain, crossed, ((1,), (1,)))
    flip = lax.rem(lax.broadcasted_iota(jnp.int32, out.shape, 0), 2) * odd
    return out * (1 - 2 * flip).astype(F32)


def four(parts, sign):
    (r0, r1, r2, r3), (i0, i1, i2, i3) = parts
    er, ei, dr, di = r0 + r2, i0 + i2, r0 - r2, i0 - i2
    fr, fi, gr, gi = r1 + r3, i1 + i3, r1 - r3, i1 - i3
    up_r, up_i = dr - gi, di + gr
    down_r, down_i = dr + gi, di - gr
    if sign < 0:
        up_r, up_i, down_r, down_i = down_r, down_i, up_r, up_i
    return (er + fr, up_r, er - fr, down_r), (ei + fi, up_i, ei - fi, down_i)


def forward_y(stress, dft, turn_y):
    parts = [[field[:, 256 * a : 256 * a + 256] for a in range(4)] for field in stress]
    real, imag = (jnp.concatenate(list(part), 0) for part in four(parts, -1))
    turned_real = turn_y[0] * real + turn_y[1] * imag
    turned_imag = turn_y[0] * imag - turn_y[1] * real
    plain = jnp.concatenate([turned_real, turned_imag], 0)
    crossed = jnp.concatenate([turned_imag, -turned_real], 0)
    return parity(dft, wide, plain, crossed, ((1,), (1,)))


def inverse_y(received, back, turn_y):
    even, odd = folded(received)
    highest = pltpu.roll(received[128:136], 64, 1) * crossing((8, 128))
    even = [first_row(received[:8], even[:8]), even[8:]]
    odd = [first_row(highest, odd[:8]), odd[8:]]
    across = jnp.concatenate(even + odd, 0).T
    odd = jnp.concatenate([-across[64:, 128:], across[:64, 128:]], 0)
    rows = jnp.concatenate([across[:, :128], odd], 1)
    both = three(halves(rows), [part[...] for part in back], ((1,), (1,)))
    real, imag = both[:64], both[64:]
    turned_real = turn_y[0] * real - turn_y[1] * imag
    turned_imag = turn_y[0] * imag + turn_y[1] * real
    parts = [
        [part[16 * j : 16 * j + 16] for j in range(4)] for part in (turned_real, turned_imag)
    ]
    return [jnp.concatenate(list(part), 1) for part in four(parts, 1)]


def local_stress(normal, shear, fraction):
    lame_field = lame_silicon + (lame_germanium - lame_silicon) * fraction
    shear_field = 2.0 * (shear_silicon + (shear_germanium - shear_silicon) * fraction)
    excess = normal - fraction
    trace = excess + pltpu.roll(excess, 4, 0)
    return lame_field * trace + shear_field * excess, shear_field * shear, excess


def dft_parts(dfts):
    dft, coarse = (
        [[dfts.at[pl.ds(at + 272 * k + start, size)] for k in range(2)] for start, size in ((0, 144), (144, 128))]
        for at in (0, 544)
    )
    return dft, coarse, [dfts.at[pl.ds(1088 + 256 * k, 256)] for k in range(2)]


def ring(steps, size):
    return min(steps % size, -steps % size)


def kernel(
    occupancy_in,
    colour_in,
    direction_in,
    barrier_in,
    dft_in,
    both_in,
    small_in,
    turn_in,
    turn_y_in,
    turn_own_in,
    strain_out,
    composition_out,
    occupancy,
    colour,
    direction,
    barrier,
    dfts,
    both,
    small,
    turn,
    turn_y,
    turn_own,
    green,
    normal,
    shear,
    fraction_pencil,
    first_sent,
    first_got,
    packed,
    landed,
    fraction_sent,
    fraction_got,
    static,
    rows_sent,
    rows_got,
    cols_sent,
    cols_got,
    corner_got,
    fields,
    strain_sent,
    strain_got,
    energy_sent,
    energy_got,
    input_sem,
    first_sem,
    send_sem,
    recv_sem,
    fraction_sem,
    halo_send,
    halo_recv,
    last_send,
    last_recv,
    edge_send,
    edge_recv,
):
    gx, gy = lax.axis_index("gx"), lax.axis_index("gy")
    me = gx * GY + gy
    z, core = lax.rem(gx // 2, 8), lax.rem(gx, 2)
    x, y = gy // 2, lax.rem(gy, 2) * 2 + gx // 16

    inputs = [
        (occupancy_in, occupancy),
        (dft_in, dfts),
        (turn_own_in.at[gy], turn_own),
        (barrier_in, barrier),
        (colour_in, colour),
        (direction_in, direction),
        (small_in, small),
        (turn_in, turn),
        (turn_y_in, turn_y),
        (both_in, both),
    ]
    inputs = [
        pltpu.make_async_copy(source, target, input_sem.at[k])
        for k, (source, target) in enumerate(inputs)
    ]
    for copy in inputs:
        copy.start()

    places = sorted(
        [(dx, dy, dc) for dx in range(4) for dy in range(4) for dc in range(2)],
        key=lambda t: -(ring(t[0], 4) + ring(t[1], 4) + 0.5 * t[2]),
    )
    bases = []
    for dx, dy, dc in places:
        x_there, y_there, c_there = lax.rem(x + dx, 4), lax.rem(y + dy, 4), lax.rem(core + dc, 2)
        bases.append((lax.rem(y_there, 2) * 16 + c_there, x_there * 2 + y_there // 2))

    def to_others(send):
        def step(i, carry):
            steps = jnp.where(lax.rem(i, 2) == 0, 4 + i // 2, 4 - (i + 1) // 2)
            z_there = lax.rem(z + steps, 8)
            for base_x, base_y in bases:
                send(base_x + 2 * z_there, base_y)
            return carry

        lax.fori_loop(0, 7, step, 0)
        for base_x, base_y in bases[:-1]:
            send(base_x + 2 * z, base_y)

    entry = pltpu.get_barrier_semaphore()
    to_others(
        lambda there_x, there_y: pl.semaphore_signal(
            entry, inc=1, device_id=(there_x, there_y), device_id_type=MESH
        )
    )

    dft, coarse, back = dft_parts(dfts)
    whole = [both.at[pl.ds(256 * k, 256)] for k in range(2)]

    for copy in inputs[:3]:
        copy.wait()
    for layer in range(2):
        static[layer] = occupancy[layer].astype(F32)
    rows = first_y([static[0], static[1]], dft, turn_own, lax.rem(gy, 2))
    first_sent[:, 0, :] = rows[:, :128]
    first_sent[:, 1, :] = rows[:, 128:]
    first_got[me] = first_sent[me]
    for there in range(GY):
        part = slice(4 * there, 4 * there + 4)
        fraction_sent[there] = jnp.concatenate([static[0, part], static[1, part]], 0)
    fraction_got[gy] = fraction_sent[gy]

    pl.semaphore_wait(entry, DEVICES - 1)

    def send_first(there_x, there_y):
        pltpu.make_async_remote_copy(
            first_sent.at[there_x * GY + there_y],
            first_got.at[me],
            first_sem.at[0],
            first_sem.at[1],
            device_id=(there_x, there_y),
            device_id_type=MESH,
        ).start()

    to_others(send_first)

    def total(source, target, send, recv, rows):
        return pltpu.make_async_remote_copy(
            source.at[pl.ds(0, rows)],
            target.at[pl.ds(0, rows)],
            send,
            recv,
            device_id=(gx + 1 - 2 * core, gy),
            device_id_type=MESH,
        )

    offsets = sorted(
        [(dx, dy) for dx in range(4) for dy in range(2) if dx + dy > 0],
        key=lambda t: -(ring(t[0], 4) + 2 * t[1]),
    )
    peers = [lax.rem(x + dx, 4) * 2 + lax.rem(gy + dy, 2) for dx, dy in offsets]

    def to_peers(source, target, send, recv):
        for there in peers:
            pltpu.make_async_remote_copy(
                source.at[there],
                target.at[gy],
                send,
                recv,
                device_id=(gx, there),
                device_id_type=MESH,
            ).start()
        return total(source, target, send, recv, GY - 1)

    fraction_copies = to_peers(fraction_sent, fraction_got, fraction_sem.at[0], fraction_sem.at[1])

    for copy in inputs[3:]:
        copy.wait()
    for layer in range(2):
        static[2 + layer] = barrier[layer]
        static[4 + layer] = colour[layer].astype(F32)
        for section in range(SECTIONS):
            static[6 + 2 * section + layer] = direction[section, layer].astype(F32)
    upper = lax.broadcasted_iota(jnp.int32, (8, COLS), 0) < 4
    for kind in range(STATIC // 2):
        one, two = static[2 * kind], static[2 * kind + 1]
        rows_sent[0, kind] = jnp.where(upper, one[:8], pltpu.roll(two[:8], 4, 0))
        rows_sent[1, kind] = jnp.where(upper, pltpu.roll(one[-8:], 4, 0), two[-8:])
    flat = [static[k] for k in range(STATIC)] + [jnp.zeros((64, COLS), F32)]
    across = jnp.concatenate(flat, 0).T
    cols_sent[0] = across[:8]
    cols_sent[1] = across[-8:]

    up, down = lax.rem(gx + 1, GX), lax.rem(gx + GX - 1, GX)
    after, before = lax.rem(gy + 1, GY), lax.rem(gy + GY - 1, GY)
    halos = [
        (rows_sent.at[0], rows_got.at[0], (down, gy)),
        (rows_sent.at[1], rows_got.at[1], (up, gy)),
        (cols_sent.at[0], cols_got.at[0], (gx, before)),
        (cols_sent.at[1], cols_got.at[1], (gx, after)),
        (cols_sent.at[0], corner_got.at[0], (down, before)),
        (cols_sent.at[1], corner_got.at[1], (down, after)),
        (cols_sent.at[0], corner_got.at[2], (up, before)),
        (cols_sent.at[1], corner_got.at[3], (up, after)),
    ]
    halos = [
        pltpu.make_async_remote_copy(
            source, target, halo_send.at[k], halo_recv.at[k], device_id=there, device_id_type=MESH
        )
        for k, (source, target, there) in enumerate(halos)
    ]
    for copy in halos:
        copy.start()
    green_tables(me, green)

    total(first_sent, first_got, first_sem.at[0], first_sem.at[1], DEVICES - 1).wait_recv()
    received = jnp.concatenate([first_got[:, 0, :], first_got[:, 1, :]], 1)

    def start_exchange(slot, rows):
        packed[slot, :, 0, :] = rows

        def send(there_x, there_y):
            pltpu.make_async_remote_copy(
                packed.at[slot, there_x * GY + there_y],
                landed.at[slot, me],
                send_sem.at[slot],
                recv_sem.at[slot],
                device_id=(there_x, there_y),
                device_id_type=MESH,
            ).start()

        to_others(send)
        landed[slot, me] = packed[slot, me]

    def exchanged(slot):
        return total(
            packed.at[slot], landed.at[slot], send_sem.at[slot], recv_sem.at[slot], DEVICES - 1
        )

    def end_exchange(slot):
        exchanged(slot).wait_recv()
        return landed[slot, :, 0, :]

    start_exchange(0, spectral_first(received, coarse, back, turn, small, green))

    fraction_copies.wait_recv()
    pencil = jnp.concatenate([fraction_got[g] for g in range(GY)], 1)
    other = pltpu.roll(pencil, 4, 0)
    upper_wide = lax.broadcasted_iota(jnp.int32, (8, POINTS), 0) < 4
    fraction_pencil[0] = jnp.where(upper_wide, pencil, other)
    fraction_pencil[1] = jnp.where(upper_wide, other, pencil)
    for copy in halos:
        copy.wait_recv()

    def side(ahead, behind):
        gap = jnp.zeros((COLS - 16, 384), F32)
        return jnp.concatenate([ahead, gap, behind], 0).T

    beside = side(cols_got[0], cols_got[1])
    below = side(corner_got[0], corner_got[1])
    above = side(corner_got[2], corner_got[3])
    for k in range(STATIC):
        kind, layer = k // 2, k % 2
        part = slice(ROWS * k, ROWS * k + ROWS)
        fields[k, :ROWS, :COLS] = static[k]
        fields[k, :ROWS, COLS:] = beside[part]
        low, high = rows_got[0, kind], rows_got[1, kind]
        if layer == 0:
            high = pltpu.roll(high, 4, 0)
        else:
            low = pltpu.roll(low, 4, 0)
        fields[k, ROWS:, :COLS] = jnp.where(upper, low, high)
        fields[k, ROWS:, COLS:] = jnp.where(upper, below[part][:8], above[part][-8:])

    change = inverse_y(end_exchange(0), back, turn_y)
    for p in range(2):
        normal[p] = change[p][:8]
        shear[p] = change[p][8:]

    def sweep(i, carry):
        stress = []
        for p in range(2):
            stress_normal, stress_shear, _ = local_stress(normal[p], shear[p], fraction_pencil[p])
            stress.append(jnp.concatenate([stress_normal, stress_shear], 0))
        start_exchange(2 * i + 1, forward_y(stress, dft, turn_y))
        arrived = end_exchange(2 * i + 1)
        start_exchange(2 * i + 2, spectral(arrived, whole, back, turn, small, green))
        change = inverse_y(end_exchange(2 * i + 2), back, turn_y)
        for p in range(2):
            normal[p] += change[p][:8]
            shear[p] += change[p][8:]
        return carry

    lax.fori_loop(0, ITERS - 1, sweep, 0)

    energies = []
    for p in range(2):
        stress_normal, stress_shear, excess = local_stress(normal[p], shear[p], fraction_pencil[p])
        density = stress_normal * excess + 2.0 * stress_shear * shear[p]
        energies.append(0.5 * (density + pltpu.roll(density, 4, 0)))
    energy = jnp.where(upper_wide, energies[0], energies[1])
    shears = jnp.where(upper_wide, shear[0], pltpu.roll(shear[1], 4, 0))
    left = lax.broadcasted_iota(jnp.int32, (8, COLS), 1) < COLS // 2

    def block(values, g):
        return values[:, COLS * (g % GY) : COLS * (g % GY) + COLS]

    for g in range(GY):
        energy_sent[g, :, :COLS] = block(energy, g)
        energy_sent[g, :, COLS:] = jnp.where(left, block(energy, g + 1), block(energy, g - 1))

    def edge_copy(g, slot, there):
        return pltpu.make_async_remote_copy(
            energy_sent.at[g],
            energy_got.at[GY + slot],
            edge_send.at[slot],
            edge_recv.at[slot],
            device_id=(there, g),
            device_id_type=MESH,
        )

    @pl.when(gy == 0)
    def _():
        for g in range(GY):
            edge_copy(g, 0, down).start()

    @pl.when(gy == GY - 1)
    def _():
        for g in range(GY):
            edge_copy(g, 1, up).start()

    energy_copies = to_peers(energy_sent, energy_got, last_send.at[0], last_recv.at[0])
    for g in range(GY):
        strain_sent[g, 0:8] = block(normal[0], g)
        strain_sent[g, 8:16] = block(normal[1], g)
        strain_sent[g, 16:24] = block(shears, g)
    strain_copies = to_peers(strain_sent, strain_got, last_send.at[1], last_recv.at[1])
    energy_got[gy] = energy_sent[gy]
    strain_got[gy] = strain_sent[gy]

    total(first_sent, first_got, first_sem.at[0], first_sem.at[1], DEVICES - 1).wait_send()
    fraction_copies.wait_send()
    for copy in halos:
        copy.wait_send()
    for slot in range(2 * ITERS - 1):
        exchanged(slot).wait_send()

    energy_copies.wait_recv()
    for slot in range(2):
        edge_copy(0, slot, up).wait_recv()
    low = lax.broadcasted_iota(jnp.int32, (8, 2 * COLS), 0) < 4

    for layer in range(2):
        pieces = []
        for pair in range(GY // 2 + 1):
            one, two = energy_got[2 * pair], energy_got[2 * pair + 1]
            if layer == 0:
                pieces.append(jnp.where(low, one, pltpu.roll(two, 4, 0)))
            else:
                pieces.append(jnp.where(low, pltpu.roll(one, 4, 0), two))
        drive = fields[2 + layer] + elastic_weight * jnp.concatenate(pieces, 0) + base_rate
        sites = fields[layer]
        tall, wide = ROWS + 8, 2 * COLS
        for section in range(SECTIONS):
            way = fields[6 + 2 * section + layer]
            above, below = pltpu.roll(sites, 1, 0), pltpu.roll(sites, tall - 1, 0)
            ahead, behind = pltpu.roll(sites, wide - 1, 1), pltpu.roll(sites, 1, 1)
            neighbours = above + below + behind + ahead
            rate = 1.0 / (1.0 + jnp.exp(bond_energy * neighbours - drive))
            target = jnp.where(
                way == 0.0,
                below,
                jnp.where(way == 1.0, above, jnp.where(way == 2.0, ahead, behind)),
            )
            flux = jnp.where(
                fields[4 + layer] == float(section), rate * sites * (1.0 - target), 0.0
            )
            parted = [jnp.where(way == float(number), flux, 0.0) for number in range(4)]
            sites = (
                sites
                - flux
                + (
                    pltpu.roll(parted[0], 1, 0)
                    + pltpu.roll(parted[1], tall - 1, 0)
                    + pltpu.roll(parted[2], 1, 1)
                    + pltpu.roll(parted[3], wide - 1, 1)
                )
            )
        composition_out[layer] = sites[:ROWS, :COLS]

    strain_copies.wait_recv()
    for g in range(GY):
        rows = slice(4 * g, 4 * g + 4)
        for layer in range(2):
            strain_out[0, layer, rows] = strain_got[g, 8 * layer : 8 * layer + 4]
            strain_out[1, layer, rows] = strain_got[g, 8 * layer + 4 : 8 * layer + 8]
            strain_out[2, layer, rows] = strain_got[g, 16 + 4 * layer : 20 + 4 * layer]

    energy_copies.wait_send()
    strain_copies.wait_send()

    @pl.when(gy == 0)
    def _():
        for g in range(GY):
            edge_copy(g, 0, down).wait_send()

    @pl.when(gy == GY - 1)
    def _():
        for g in range(GY):
            edge_copy(g, 1, up).wait_send()


def on_device(occupancy, colour, hop_direction, barrier):
    operands = (occupancy, colour, hop_direction, barrier) + tuple(
        jnp.asarray(table) for table in tables()
    )
    vmem = pl.BlockSpec(memory_space=pltpu.VMEM)
    dma = pltpu.SemaphoreType.DMA
    exchanges = 2 * ITERS - 1
    return pl.pallas_call(
        kernel,
        out_shape=(
            jax.ShapeDtypeStruct((3, 2, ROWS, COLS), F32),
            jax.ShapeDtypeStruct((2, ROWS, COLS), F32),
        ),
        in_specs=[pl.BlockSpec(memory_space=pltpu.HBM)] * len(operands),
        out_specs=(vmem, vmem),
        scratch_shapes=[
            pltpu.VMEM((2, ROWS, COLS), jnp.int32),
            pltpu.VMEM((2, ROWS, COLS), jnp.int32),
            pltpu.VMEM((2, 2, ROWS, COLS), jnp.int32),
            pltpu.VMEM((2, ROWS, COLS), F32),
            pltpu.VMEM((1600, 256), BF16),
            pltpu.VMEM((512, 512), BF16),
            pltpu.VMEM((128, 896), BF16),
            pltpu.VMEM((4, 256, 128), F32),
            pltpu.VMEM((2, 64, 256), F32),
            pltpu.VMEM((2, 16, COLS), F32),
            pltpu.VMEM((3, 256, 128), F32),
            pltpu.VMEM((2, 8, POINTS), F32),
            pltpu.VMEM((2, 8, POINTS), F32),
            pltpu.VMEM((2, 8, POINTS), F32),
            pltpu.VMEM((DEVICES, 2, 128), F32),
            pltpu.VMEM((DEVICES, 2, 128), F32),
            pltpu.VMEM((exchanges, DEVICES, 1, 128), F32),
            pltpu.VMEM((exchanges, DEVICES, 1, 128), F32),
            pltpu.VMEM((GY, 8, COLS), F32),
            pltpu.VMEM((GY, 8, COLS), F32),
            pltpu.VMEM((STATIC, ROWS, COLS), F32),
            pltpu.VMEM((2, STATIC // 2, 8, COLS), F32),
            pltpu.VMEM((2, STATIC // 2, 8, COLS), F32),
            pltpu.VMEM((2, 8, 384), F32),
            pltpu.VMEM((2, 8, 384), F32),
            pltpu.VMEM((4, 8, 384), F32),
            pltpu.VMEM((STATIC, ROWS + 8, 2 * COLS), F32),
            pltpu.VMEM((GY, 24, COLS), F32),
            pltpu.VMEM((GY, 24, COLS), F32),
            pltpu.VMEM((GY, 8, 2 * COLS), F32),
            pltpu.VMEM((GY + 2, 8, 2 * COLS), F32),
            dma((10,)),
            dma((2,)),
            dma((exchanges,)),
            dma((exchanges,)),
            dma((2,)),
            dma((8,)),
            dma((8,)),
            dma((2,)),
            dma((2,)),
            dma((2,)),
            dma((2,)),
        ],
        compiler_params=pltpu.CompilerParams(
            collective_id=0, has_side_effects=True, vmem_limit_bytes=40 * 1024 * 1024
        ),
        name="film",
    )(*[pltpu.with_memory_space_constraint(x, pltpu.HBM) for x in operands])


def solution(mesh):
    placed = (
        P(None, "gx", "gy"),
        P(None, "gx", "gy"),
        P(None, None, "gx", "gy"),
        P(None, "gx", "gy"),
    )
    return jax.shard_map(
        on_device,
        mesh=mesh,
        in_specs=placed,
        out_specs=(P(None, None, "gx", "gy"), P(None, "gx", "gy")),
        check_vma=False,
    )
```

```python
import functools
import math

import jax
import jax.numpy as jnp
import ml_dtypes
import numpy as np
from jax import lax
from jax.experimental import pallas as pl
from jax.experimental.pallas import tpu as pltpu
from jax.sharding import PartitionSpec as P

MESH = pl.DeviceIdType.MESH
F32 = jnp.float32
BF16 = jnp.bfloat16

ITERS = 3
SECTIONS = 2
GX, GY = 32, 8
DEVICES = GX * GY
POINTS = 1024
ROWS, COLS = POINTS // GX, POINTS // GY
STATIC = 10

lame_silicon = 1.2
lame_germanium = 0.9
shear_silicon = 1.0
shear_germanium = 0.8
lame_medium = 1.05
shear_medium = 0.9
elastic_weight = 2.0
bond_energy = 0.7
base_rate = 1.0


def split(values):
    high = values.astype(ml_dtypes.bfloat16)
    return high, (values - high.astype(np.float64)).astype(ml_dtypes.bfloat16)


def waves(angle, axis):
    return np.concatenate([np.cos(angle), np.sin(angle)], axis)


def half_waves(angle):
    return np.concatenate([np.cos(angle[:144]), np.sin(angle[:128])], 0)


def tables():
    index = np.arange(256)
    angle = 2 * np.pi * (np.outer(index, index) % 256) / 256
    coarse = np.concatenate([index[:32], -index[:32] % 32])
    coarse = 2 * np.pi * (np.outer(coarse, index // 8) % 32) / 32
    order = np.concatenate([index[:129], 384 - index[129:]])
    both = np.concatenate([np.cos(angle[order]), np.sin(angle[order])], 1)
    back = np.concatenate([np.cos(angle[:, :128]), np.sin(angle[:, :128])], 1)
    back[:, 128] = np.cos(angle[:, 128])
    dft = split(half_waves(angle)) + split(waves(coarse, 0)) + split(back)
    lane = np.arange(128)
    turn_x = waves(2 * np.pi * np.outer(order, lane % 4) / POINTS, 0)
    turn_first = waves(2 * np.pi * np.outer(order, lane // 16 * 4 + lane % 4) / POINTS, 0)
    turn_y = waves(2 * np.pi * np.outer(np.arange(64) // 16, index) / POINTS, 0).reshape(2, 64, 256)
    stress = -2.0 * (lame_germanium + shear_germanium)
    angle = 2 * np.pi * np.outer(np.arange(16) // 4, np.arange(POINTS)) / POINTS
    turn_own = stress * np.stack([np.cos(angle), np.sin(angle)])
    turn_own = turn_own.reshape(2, 16, GY, COLS).transpose(2, 0, 1, 3)
    part, freq, comp, quad = lane // 64, lane // 16 % 4, lane // 4 % 4, lane % 4
    turns = np.outer(quad, quad) % 4
    cos4, sin4 = np.array([1, 0, -1, 0])[turns], np.array([0, 1, 0, -1])[turns]
    same_freq = freq[:, None] == freq[None, :]
    same_part = part[:, None] == part[None, :]
    to_real = part[None, :] == 0
    used = (comp[None, :] < 3) & same_freq
    forward = np.where(same_part, cos4, np.where(to_real, sin4, -sin4))
    forward4 = np.concatenate([forward * (used & (comp[:, None] == c)) for c in range(3)], 1)
    inverse = np.where(same_part, cos4, np.where(to_real, -sin4, sin4))
    inverse = inverse * (used & (comp[:, None] == comp[None, :]))
    turned = np.concatenate([-inverse[:, 64:], inverse[:, :64]], 1)
    inverse4 = np.concatenate([inverse, turned], 1)
    first4 = np.where((comp == 0)[:, None], forward4[:, :128], 0)
    picked = np.zeros((256, 128))
    for p in range(2):
        for n in range(128):
            picked[p * 128 + n] = first4[p * 64 + n // 4 % 4 * 16 + n % 4]
    both = np.concatenate(split(both), 0)
    small = np.concatenate([forward4, inverse4, picked[:128], picked[128:]], 1)
    return (
        np.concatenate(dft, 0),
        both,
        small.astype(ml_dtypes.bfloat16),
        np.concatenate([turn_x, turn_first], 0).reshape(4, 256, 128).astype(np.float32),
        turn_y.astype(np.float32),
        turn_own.astype(np.float32),
    )


def halves(values):
    high = values.astype(BF16)
    return high, (values - high.astype(F32)).astype(BF16)


def dot(left, right, dims):
    return lax.dot_general(left, right, (dims, ((), ())), preferred_element_type=F32)


def wide(table, values, dims):
    high, low = halves(values)
    both = dot(table[0][...], jnp.concatenate([high, low], 1 - dims[1][0]), dims)
    return both[:, :128] + both[:, 128:] + dot(table[1][...], high, dims)


def narrow(table, values, dims):
    return three([part[...] for part in table], halves(values), dims)


def parity(dft, multiply, plain, crossed, dims):
    even, odd = multiply(dft[0], plain, dims), multiply(dft[1], crossed, dims)
    minus = even[:128] - odd
    return jnp.concatenate(
        [even[:128] + odd, first_row(even[128:136], minus[:8]), minus[8:]], 0
    )


def first_row(special, others):
    return jnp.where(lax.broadcasted_iota(jnp.int32, others.shape, 0) == 0, special, others)


def folded(values):
    return values[:128] + values[128:], values[:128] - values[128:]


def three(left, right, dims):
    return dot(left[0], right[0], dims) + dot(left[0], right[1], dims) + dot(left[1], right[0], dims)


def exact(values, table):
    return dot(jnp.concatenate(halves(values), 1), jnp.concatenate([table, table], 0), ((1,), (0,)))


def green_tables(device, green):
    shape = (256, 128)
    lane = lax.broadcasted_iota(jnp.int32, shape, 1)
    comp = lax.rem(lane // 4, 4)
    row = lax.broadcasted_iota(jnp.int32, shape, 0)
    index_x = jnp.where(row > 128, 384 - row, row) + 256 * lax.rem(lane, 4)
    index_y = 4 * jnp.where(device > 128, 384 - device, device) + lax.rem(lane // 16, 4)
    unit = 2.0 * math.pi / POINTS
    a = jnp.where(index_x < POINTS // 2, index_x, index_x - POINTS).astype(F32) * unit
    b = jnp.where(index_y < POINTS // 2, index_y, index_y - POINTS).astype(F32) * unit
    ratio = (lame_medium + shear_medium) / (lame_medium + 2.0 * shear_medium)
    squared = a * a + b * b
    positive = squared > 0
    inverse_sq = jnp.where(positive, 1.0 / jnp.where(positive, squared, 1.0), 0.0)
    base = inverse_sq * (-1.0 / (shear_medium * POINTS * POINTS))
    edge_x = (index_x == POINTS // 2).astype(F32)
    edge_y = (index_y == POINTS // 2).astype(F32)
    odd = base * (1.0 - jnp.abs(edge_x - edge_y))
    aa, bb, ab = a * a, b * b, a * b
    xx_xx = (aa - ratio * aa * aa * inverse_sq) * base
    yy_yy = (bb - ratio * bb * bb * inverse_sq) * base
    xx_yy = -ratio * aa * bb * inverse_sq * base
    xx_xy = (ab - 2.0 * ratio * aa * ab * inverse_sq) * odd
    yy_xy = (ab - 2.0 * ratio * bb * ab * inverse_sq) * odd
    xy_xy = 0.5 * (aa + bb - 4.0 * ratio * aa * bb * inverse_sq) * base

    def pick(first, second, third):
        return jnp.where(
            comp == 0, first, jnp.where(comp == 1, second, jnp.where(comp == 2, third, 0.0))
        )

    green[0] = pick(xx_xx, xx_yy, 0.5 * xx_xy)
    green[1] = pick(xx_yy, yy_yy, 0.5 * yy_xy)
    green[2] = pick(xx_xy, yy_xy, xy_xy)


def crossing(shape):
    return jnp.where(lax.broadcasted_iota(jnp.int32, shape, 1) < 64, 1.0, -1.0)


def spectral(received, dft, back, turn, small, green):
    sign = crossing((256, 128))
    swapped = pltpu.roll(received, 64, 1) * sign
    first = wide(dft, jnp.concatenate([received, swapped], 0), ((1,), (0,)))
    turned = turn[0] * first + turn[1] * (pltpu.roll(first, 64, 1) * sign)
    spread = exact(turned, small[:, :384])
    mapped = (
        green[0] * spread[:, :128] + green[1] * spread[:, 128:256] + green[2] * spread[:, 256:]
    )
    return spectral_back(mapped, back, turn, small)


def spectral_back(mapped, back, turn, small):
    both = exact(mapped, small[:, 384:640])
    plain, crossed = both[:, :128], both[:, 128:]
    values = turn[0] * plain + turn[1] * crossed
    crossed = turn[0] * crossed - turn[1] * plain
    even, odd = folded(values)[0], folded(crossed)[1]
    even = [first_row(values[:8], even[:8]), even[8:]]
    odd = [first_row(values[128:136], odd[:8]), odd[8:]]
    return wide(back, jnp.concatenate(even + odd, 0), ((1,), (0,)))


def spectral_first(received, coarse, back, turn, small, green):
    both = three([part[...] for part in coarse], halves(received), ((1,), (0,)))
    cos, sin = both[:64], both[64:]
    real, imag = (
        jnp.concatenate([part[:32]] * 4 + [part[32:]] * 4, 0)
        for part in (cos[:, :128] + sin[:, 128:], cos[:, 128:] - sin[:, :128])
    )
    real, imag = turn[2] * real + turn[3] * imag, turn[2] * imag - turn[3] * real
    spread = exact(
        jnp.concatenate([real, imag], 1),
        jnp.concatenate([small[:, 640:768], small[:, 768:896]], 0),
    )
    return spectral_back((green[0] + green[1]) * spread, back, turn, small)


def first_y(fields, dft, turn, odd):
    upper = lax.broadcasted_iota(jnp.int32, (8, COLS), 0) < 4
    spread = []
    for field in fields:
        pieces = []
        for t in range(ROWS // 8):
            tile = field[8 * t : 8 * t + 8]
            other = pltpu.roll(tile, 4, 0)
            one, two = jnp.where(upper, tile, other), jnp.where(upper, other, tile)
            pieces += [one, one, two, two]
        spread.append(jnp.concatenate(pieces, 0))
    real, imag = spread
    cos, sin = (jnp.concatenate([turn[k]] * 8, 0) for k in range(2))
    real, imag = cos * real + sin * imag, cos * imag - sin * real
    plain, crossed = jnp.concatenate([real, imag], 0), jnp.concatenate([imag, -real], 0)
    table = [[part.at[:, pl.ds(0, 128)] for part in parts] for parts in dft]
    out = parity(table, narrow, plain, crossed, ((1,), (1,)))
    flip = lax.rem(lax.broadcasted_iota(jnp.int32, out.shape, 0), 2) * odd
    return out * (1 - 2 * flip).astype(F32)


def four(parts, sign):
    (r0, r1, r2, r3), (i0, i1, i2, i3) = parts
    er, ei, dr, di = r0 + r2, i0 + i2, r0 - r2, i0 - i2
    fr, fi, gr, gi = r1 + r3, i1 + i3, r1 - r3, i1 - i3
    up_r, up_i = dr - gi, di + gr
    down_r, down_i = dr + gi, di - gr
    if sign < 0:
        up_r, up_i, down_r, down_i = down_r, down_i, up_r, up_i
    return (er + fr, up_r, er - fr, down_r), (ei + fi, up_i, ei - fi, down_i)


def forward_y(stress, dft, turn_y):
    parts = [[field[:, 256 * a : 256 * a + 256] for a in range(4)] for field in stress]
    real, imag = (jnp.concatenate(list(part), 0) for part in four(parts, -1))
    turned_real = turn_y[0] * real + turn_y[1] * imag
    turned_imag = turn_y[0] * imag - turn_y[1] * real
    plain = jnp.concatenate([turned_real, turned_imag], 0)
    crossed = jnp.concatenate([turned_imag, -turned_real], 0)
    return parity(dft, wide, plain, crossed, ((1,), (1,)))


def inverse_y(received, back, turn_y):
    even, odd = folded(received)
    highest = pltpu.roll(received[128:136], 64, 1) * crossing((8, 128))
    even = [first_row(received[:8], even[:8]), even[8:]]
    odd = [first_row(highest, odd[:8]), odd[8:]]
    across = jnp.concatenate(even + odd, 0).T
    odd = jnp.concatenate([-across[64:, 128:], across[:64, 128:]], 0)
    rows = jnp.concatenate([across[:, :128], odd], 1)
    both = three(halves(rows), [part[...] for part in back], ((1,), (1,)))
    real, imag = both[:64], both[64:]
    turned_real = turn_y[0] * real - turn_y[1] * imag
    turned_imag = turn_y[0] * imag + turn_y[1] * real
    parts = [
        [part[16 * j : 16 * j + 16] for j in range(4)] for part in (turned_real, turned_imag)
    ]
    return [jnp.concatenate(list(part), 1) for part in four(parts, 1)]


def local_stress(normal, shear, fraction):
    lame_field = lame_silicon + (lame_germanium - lame_silicon) * fraction
    shear_field = 2.0 * (shear_silicon + (shear_germanium - shear_silicon) * fraction)
    excess = normal - fraction
    trace = excess + pltpu.roll(excess, 4, 0)
    return lame_field * trace + shear_field * excess, shear_field * shear, excess


def dft_parts(dfts):
    def rows(at, step, size):
        return [dfts.at[pl.ds(at + step * k, size)] for k in range(2)]

    return [rows(0, 272, 144), rows(144, 272, 128)], rows(544, 128, 128), rows(800, 256, 256)


def ring(steps, size):
    return min(steps % size, -steps % size)


def kernel(
    occupancy_in,
    colour_in,
    direction_in,
    barrier_in,
    dft_in,
    both_in,
    small_in,
    turn_in,
    turn_y_in,
    turn_own_in,
    strain_out,
    composition_out,
    occupancy,
    colour,
    direction,
    barrier,
    dfts,
    both,
    small,
    turn,
    turn_y,
    turn_own,
    green,
    normal,
    shear,
    fraction_pencil,
    first_sent,
    first_got,
    packed,
    landed,
    fraction_sent,
    fraction_got,
    static,
    rows_sent,
    rows_got,
    cols_sent,
    cols_got,
    corner_got,
    fields,
    strain_sent,
    strain_got,
    energy_sent,
    energy_got,
    input_sem,
    first_sem,
    send_sem,
    recv_sem,
    fraction_sem,
    halo_send,
    halo_recv,
    last_send,
    last_recv,
    edge_send,
    edge_recv,
):
    gx, gy = lax.axis_index("gx"), lax.axis_index("gy")
    me = gx * GY + gy
    z, core = lax.rem(gx // 2, 8), lax.rem(gx, 2)
    x, y = gy // 2, lax.rem(gy, 2) * 2 + gx // 16

    inputs = [
        (occupancy_in, occupancy),
        (dft_in, dfts),
        (turn_own_in.at[gy], turn_own),
        (barrier_in, barrier),
        (colour_in, colour),
        (direction_in, direction),
        (small_in, small),
        (turn_in, turn),
        (turn_y_in, turn_y),
        (both_in, both),
    ]
    inputs = [
        pltpu.make_async_copy(source, target, input_sem.at[k])
        for k, (source, target) in enumerate(inputs)
    ]
    x_part = [lax.rem(x + dx, 4) * 2 for dx in range(4)]
    y_part = [lax.rem(y + dy, 4) for dy in range(4)]
    y_part = [(lax.rem(there, 2) * 16, there // 2) for there in y_part]
    c_part = [core, 1 - core]
    groups = [[] for _ in range(5)]
    for dx in range(4):
        for dy in range(4):
            for dc in (1, 0):
                there = (y_part[dy][0] + c_part[dc], x_part[dx] + y_part[dy][1])
                groups[ring(dx, 4) + ring(dy, 4)].append(there)

    def to_others(send):
        def at(z_there, places):
            for gx_part, gy_there in places:
                send(gx_part + 2 * z_there, gy_there)

        def step(i, carry):
            for hops in (4, 3, 2, 1, 0):
                along_z = 8 - i - hops
                up_z, down_z = lax.rem(z + along_z + 8, 8), lax.rem(z - along_z + 8, 8)
                within = (along_z >= 0) & (along_z <= 4)
                if hops > 0:
                    pl.when(within)(functools.partial(at, up_z, groups[hops]))
                else:
                    pl.when(within)(functools.partial(at, up_z, groups[0][:1]))
                    pl.when((along_z >= 1) & within)(functools.partial(at, up_z, groups[0][1:]))
                pl.when((along_z >= 1) & (along_z <= 3))(
                    functools.partial(at, down_z, groups[hops])
                )
            return carry

        lax.fori_loop(0, 9, step, 0)

    entry = pltpu.get_barrier_semaphore()
    to_others(
        lambda there_x, there_y: pl.semaphore_signal(
            entry, inc=1, device_id=(there_x, there_y), device_id_type=MESH
        )
    )

    for copy in inputs:
        copy.start()

    dft, coarse, back = dft_parts(dfts)
    whole = [both.at[pl.ds(256 * k, 256)] for k in range(2)]

    for copy in inputs[:3]:
        copy.wait()
    for layer in range(2):
        static[layer] = occupancy[layer].astype(F32)
    rows = first_y([static[0], static[1]], dft, turn_own, lax.rem(gy, 2))
    first_sent[:, 0, :] = rows[:, :128]
    first_sent[:, 1, :] = rows[:, 128:]
    first_got[me] = first_sent[me]
    for there in range(GY):
        part = slice(4 * there, 4 * there + 4)
        fraction_sent[there] = jnp.concatenate([static[0, part], static[1, part]], 0)
    fraction_got[gy] = fraction_sent[gy]

    pl.semaphore_wait(entry, DEVICES - 1)

    def send_first(there_x, there_y):
        pltpu.make_async_remote_copy(
            first_sent.at[there_x * GY + there_y],
            first_got.at[me],
            first_sem.at[0],
            first_sem.at[1],
            device_id=(there_x, there_y),
            device_id_type=MESH,
        ).start()

    to_others(send_first)

    def total(source, target, send, recv, rows):
        return pltpu.make_async_remote_copy(
            source.at[pl.ds(0, rows)],
            target.at[pl.ds(0, rows)],
            send,
            recv,
            device_id=(gx + 1 - 2 * core, gy),
            device_id_type=MESH,
        )

    offsets = sorted(
        [(dx, dy) for dx in range(4) for dy in range(2) if dx + dy > 0],
        key=lambda t: -(ring(t[0], 4) + 2 * t[1]),
    )
    peers = [lax.rem(x + dx, 4) * 2 + lax.rem(gy + dy, 2) for dx, dy in offsets]

    def to_peers(source, target, send, recv):
        for there in peers:
            pltpu.make_async_remote_copy(
                source.at[there],
                target.at[gy],
                send,
                recv,
                device_id=(gx, there),
                device_id_type=MESH,
            ).start()
        return total(source, target, send, recv, GY - 1)

    fraction_copies = to_peers(fraction_sent, fraction_got, fraction_sem.at[0], fraction_sem.at[1])

    for copy in inputs[3:]:
        copy.wait()
    for layer in range(2):
        static[2 + layer] = barrier[layer]
        static[4 + layer] = colour[layer].astype(F32)
        for section in range(SECTIONS):
            static[6 + 2 * section + layer] = direction[section, layer].astype(F32)
    upper = lax.broadcasted_iota(jnp.int32, (8, COLS), 0) < 4
    for kind in range(STATIC // 2):
        one, two = static[2 * kind], static[2 * kind + 1]
        rows_sent[0, kind] = jnp.where(upper, one[:8], pltpu.roll(two[:8], 4, 0))
        rows_sent[1, kind] = jnp.where(upper, pltpu.roll(one[-8:], 4, 0), two[-8:])
    flat = [static[k] for k in range(STATIC)] + [jnp.zeros((64, COLS), F32)]
    across = jnp.concatenate(flat, 0).T
    cols_sent[0] = across[:8]
    cols_sent[1] = across[-8:]

    up, down = lax.rem(gx + 1, GX), lax.rem(gx + GX - 1, GX)
    after, before = lax.rem(gy + 1, GY), lax.rem(gy + GY - 1, GY)
    halos = [
        (rows_sent.at[0], rows_got.at[0], (down, gy)),
        (rows_sent.at[1], rows_got.at[1], (up, gy)),
        (cols_sent.at[0], cols_got.at[0], (gx, before)),
        (cols_sent.at[1], cols_got.at[1], (gx, after)),
        (cols_sent.at[0], corner_got.at[0], (down, before)),
        (cols_sent.at[1], corner_got.at[1], (down, after)),
        (cols_sent.at[0], corner_got.at[2], (up, before)),
        (cols_sent.at[1], corner_got.at[3], (up, after)),
    ]
    halos = [
        pltpu.make_async_remote_copy(
            source, target, halo_send.at[k], halo_recv.at[k], device_id=there, device_id_type=MESH
        )
        for k, (source, target, there) in enumerate(halos)
    ]
    for copy in halos:
        copy.start()
    green_tables(me, green)

    total(first_sent, first_got, first_sem.at[0], first_sem.at[1], DEVICES - 1).wait_recv()
    received = jnp.concatenate([first_got[:, 0, :], first_got[:, 1, :]], 1)

    def start_exchange(slot, rows):
        packed[slot, :, 0, :] = rows

        def send(there_x, there_y):
            pltpu.make_async_remote_copy(
                packed.at[slot, there_x * GY + there_y],
                landed.at[slot, me],
                send_sem.at[slot],
                recv_sem.at[slot],
                device_id=(there_x, there_y),
                device_id_type=MESH,
            ).start()

        to_others(send)
        landed[slot, me] = packed[slot, me]

    def exchanged(slot):
        return total(
            packed.at[slot], landed.at[slot], send_sem.at[slot], recv_sem.at[slot], DEVICES - 1
        )

    def end_exchange(slot):
        exchanged(slot).wait_recv()
        return landed[slot, :, 0, :]

    start_exchange(0, spectral_first(received, coarse, back, turn, small, green))

    fraction_copies.wait_recv()
    pencil = jnp.concatenate([fraction_got[g] for g in range(GY)], 1)
    other = pltpu.roll(pencil, 4, 0)
    upper_wide = lax.broadcasted_iota(jnp.int32, (8, POINTS), 0) < 4
    fraction_pencil[0] = jnp.where(upper_wide, pencil, other)
    fraction_pencil[1] = jnp.where(upper_wide, other, pencil)
    for copy in halos:
        copy.wait_recv()

    def side(ahead, behind):
        gap = jnp.zeros((COLS - 16, 384), F32)
        return jnp.concatenate([ahead, gap, behind], 0).T

    beside = side(cols_got[0], cols_got[1])
    below = side(corner_got[0], corner_got[1])
    above = side(corner_got[2], corner_got[3])
    for k in range(STATIC):
        kind, layer = k // 2, k % 2
        part = slice(ROWS * k, ROWS * k + ROWS)
        fields[k, :ROWS, :COLS] = static[k]
        fields[k, :ROWS, COLS:] = beside[part]
        low, high = rows_got[0, kind], rows_got[1, kind]
        if layer == 0:
            high = pltpu.roll(high, 4, 0)
        else:
            low = pltpu.roll(low, 4, 0)
        fields[k, ROWS:, :COLS] = jnp.where(upper, low, high)
        fields[k, ROWS:, COLS:] = jnp.where(upper, below[part][:8], above[part][-8:])

    change = inverse_y(end_exchange(0), back, turn_y)
    for p in range(2):
        normal[p] = change[p][:8]
        shear[p] = change[p][8:]

    def sweep(i, carry):
        stress = []
        for p in range(2):
            stress_normal, stress_shear, _ = local_stress(normal[p], shear[p], fraction_pencil[p])
            stress.append(jnp.concatenate([stress_normal, stress_shear], 0))
        start_exchange(2 * i + 1, forward_y(stress, dft, turn_y))
        arrived = end_exchange(2 * i + 1)
        start_exchange(2 * i + 2, spectral(arrived, whole, back, turn, small, green))
        change = inverse_y(end_exchange(2 * i + 2), back, turn_y)
        for p in range(2):
            normal[p] += change[p][:8]
            shear[p] += change[p][8:]
        return carry

    lax.fori_loop(0, ITERS - 1, sweep, 0)

    energies = []
    for p in range(2):
        stress_normal, stress_shear, excess = local_stress(normal[p], shear[p], fraction_pencil[p])
        density = stress_normal * excess + 2.0 * stress_shear * shear[p]
        energies.append(0.5 * (density + pltpu.roll(density, 4, 0)))
    energy = jnp.where(upper_wide, energies[0], energies[1])
    shears = jnp.where(upper_wide, shear[0], pltpu.roll(shear[1], 4, 0))
    left = lax.broadcasted_iota(jnp.int32, (8, COLS), 1) < COLS // 2

    def block(values, g):
        return values[:, COLS * (g % GY) : COLS * (g % GY) + COLS]

    for g in range(GY):
        energy_sent[g, :, :COLS] = block(energy, g)
        energy_sent[g, :, COLS:] = jnp.where(left, block(energy, g + 1), block(energy, g - 1))

    def edge_copy(g, slot, there):
        return pltpu.make_async_remote_copy(
            energy_sent.at[g],
            energy_got.at[GY + slot],
            edge_send.at[slot],
            edge_recv.at[slot],
            device_id=(there, g),
            device_id_type=MESH,
        )

    @pl.when(gy == 0)
    def _():
        for g in range(GY):
            edge_copy(g, 0, down).start()

    @pl.when(gy == GY - 1)
    def _():
        for g in range(GY):
            edge_copy(g, 1, up).start()

    energy_copies = to_peers(energy_sent, energy_got, last_send.at[0], last_recv.at[0])
    for g in range(GY):
        strain_sent[g, 0:8] = block(normal[0], g)
        strain_sent[g, 8:16] = block(normal[1], g)
        strain_sent[g, 16:24] = block(shears, g)
    strain_copies = to_peers(strain_sent, strain_got, last_send.at[1], last_recv.at[1])
    energy_got[gy] = energy_sent[gy]
    strain_got[gy] = strain_sent[gy]

    total(first_sent, first_got, first_sem.at[0], first_sem.at[1], DEVICES - 1).wait_send()
    fraction_copies.wait_send()
    for copy in halos:
        copy.wait_send()
    for slot in range(2 * ITERS - 1):
        exchanged(slot).wait_send()

    low = lax.broadcasted_iota(jnp.int32, (8, 2 * COLS), 0) < 4
    tall, wide_cols = ROWS + 8, 2 * COLS

    def prepared(sites, layer, section):
        way = fields[6 + 2 * section + layer]
        above, below = pltpu.roll(sites, 1, 0), pltpu.roll(sites, tall - 1, 0)
        ahead, behind = pltpu.roll(sites, wide_cols - 1, 1), pltpu.roll(sites, 1, 1)
        neighbours = above + below + behind + ahead
        target = jnp.where(
            way == 0.0,
            below,
            jnp.where(way == 1.0, above, jnp.where(way == 2.0, ahead, behind)),
        )
        moving = jnp.where(
            fields[4 + layer] == float(section), sites * (1.0 - target), 0.0
        )
        return bond_energy * neighbours - (fields[2 + layer] + base_rate), moving

    def hop(sites, ready, energy, layer, section):
        flux = ready[1] / (1.0 + jnp.exp(ready[0] - elastic_weight * energy))
        way = fields[6 + 2 * section + layer]
        parted = [jnp.where(way == float(number), flux, 0.0) for number in range(4)]
        return (
            sites
            - flux
            + (
                pltpu.roll(parted[0], 1, 0)
                + pltpu.roll(parted[1], tall - 1, 0)
                + pltpu.roll(parted[2], 1, 1)
                + pltpu.roll(parted[3], wide_cols - 1, 1)
            )
        )

    ready = [prepared(fields[layer], layer, 0) for layer in range(2)]

    energy_copies.wait_recv()
    for slot in range(2):
        edge_copy(0, slot, up).wait_recv()

    for layer in range(2):
        pieces = []
        for pair in range(GY // 2 + 1):
            one, two = energy_got[2 * pair], energy_got[2 * pair + 1]
            if layer == 0:
                pieces.append(jnp.where(low, one, pltpu.roll(two, 4, 0)))
            else:
                pieces.append(jnp.where(low, pltpu.roll(one, 4, 0), two))
        energy_here = jnp.concatenate(pieces, 0)
        sites = hop(fields[layer], ready[layer], energy_here, layer, 0)
        for section in range(1, SECTIONS):
            sites = hop(sites, prepared(sites, layer, section), energy_here, layer, section)
        composition_out[layer] = sites[:ROWS, :COLS]

    strain_copies.wait_recv()
    for g in range(GY):
        rows = slice(4 * g, 4 * g + 4)
        for layer in range(2):
            strain_out[0, layer, rows] = strain_got[g, 8 * layer : 8 * layer + 4]
            strain_out[1, layer, rows] = strain_got[g, 8 * layer + 4 : 8 * layer + 8]
            strain_out[2, layer, rows] = strain_got[g, 16 + 4 * layer : 20 + 4 * layer]

    energy_copies.wait_send()
    strain_copies.wait_send()

    @pl.when(gy == 0)
    def _():
        for g in range(GY):
            edge_copy(g, 0, down).wait_send()

    @pl.when(gy == GY - 1)
    def _():
        for g in range(GY):
            edge_copy(g, 1, up).wait_send()


def on_device(occupancy, colour, hop_direction, barrier):
    operands = (occupancy, colour, hop_direction, barrier) + tuple(
        jnp.asarray(table) for table in tables()
    )
    vmem = pl.BlockSpec(memory_space=pltpu.VMEM)
    dma = pltpu.SemaphoreType.DMA
    exchanges = 2 * ITERS - 1
    return pl.pallas_call(
        kernel,
        out_shape=(
            jax.ShapeDtypeStruct((3, 2, ROWS, COLS), F32),
            jax.ShapeDtypeStruct((2, ROWS, COLS), F32),
        ),
        in_specs=[pl.BlockSpec(memory_space=pltpu.HBM)] * len(operands),
        out_specs=(vmem, vmem),
        scratch_shapes=[
            pltpu.VMEM((2, ROWS, COLS), jnp.int32),
            pltpu.VMEM((2, ROWS, COLS), jnp.int32),
            pltpu.VMEM((2, 2, ROWS, COLS), jnp.int32),
            pltpu.VMEM((2, ROWS, COLS), F32),
            pltpu.VMEM((1312, 256), BF16),
            pltpu.VMEM((512, 512), BF16),
            pltpu.VMEM((128, 896), BF16),
            pltpu.VMEM((4, 256, 128), F32),
            pltpu.VMEM((2, 64, 256), F32),
            pltpu.VMEM((2, 16, COLS), F32),
            pltpu.VMEM((3, 256, 128), F32),
            pltpu.VMEM((2, 8, POINTS), F32),
            pltpu.VMEM((2, 8, POINTS), F32),
            pltpu.VMEM((2, 8, POINTS), F32),
            pltpu.VMEM((DEVICES, 2, 128), F32),
            pltpu.VMEM((DEVICES, 2, 128), F32),
            pltpu.VMEM((exchanges, DEVICES, 1, 128), F32),
            pltpu.VMEM((exchanges, DEVICES, 1, 128), F32),
            pltpu.VMEM((GY, 8, COLS), F32),
            pltpu.VMEM((GY, 8, COLS), F32),
            pltpu.VMEM((STATIC, ROWS, COLS), F32),
            pltpu.VMEM((2, STATIC // 2, 8, COLS), F32),
            pltpu.VMEM((2, STATIC // 2, 8, COLS), F32),
            pltpu.VMEM((2, 8, 384), F32),
            pltpu.VMEM((2, 8, 384), F32),
            pltpu.VMEM((4, 8, 384), F32),
            pltpu.VMEM((STATIC, ROWS + 8, 2 * COLS), F32),
            pltpu.VMEM((GY, 24, COLS), F32),
            pltpu.VMEM((GY, 24, COLS), F32),
            pltpu.VMEM((GY, 8, 2 * COLS), F32),
            pltpu.VMEM((GY + 2, 8, 2 * COLS), F32),
            dma((10,)),
            dma((2,)),
            dma((exchanges,)),
            dma((exchanges,)),
            dma((2,)),
            dma((8,)),
            dma((8,)),
            dma((2,)),
            dma((2,)),
            dma((2,)),
            dma((2,)),
        ],
        compiler_params=pltpu.CompilerParams(
            collective_id=0, has_side_effects=True, vmem_limit_bytes=40 * 1024 * 1024
        ),
        name="film",
    )(*[pltpu.with_memory_space_constraint(x, pltpu.HBM) for x in operands])


def solution(mesh):
    placed = (
        P(None, "gx", "gy"),
        P(None, "gx", "gy"),
        P(None, None, "gx", "gy"),
        P(None, "gx", "gy"),
    )
    return jax.shard_map(
        on_device,
        mesh=mesh,
        in_specs=placed,
        out_specs=(P(None, None, "gx", "gy"), P(None, "gx", "gy")),
        check_vma=False,
    )
```

```python
import functools
import math

import jax
import jax.numpy as jnp
import ml_dtypes
import numpy as np
from jax import lax
from jax.experimental import pallas as pl
from jax.experimental.pallas import tpu as pltpu
from jax.sharding import PartitionSpec as P

MESH = pl.DeviceIdType.MESH
F32 = jnp.float32
BF16 = jnp.bfloat16

ITERS = 3
SECTIONS = 2
GX, GY = 32, 8
DEVICES = GX * GY
POINTS = 1024
ROWS, COLS = POINTS // GX, POINTS // GY
STATIC = 10

lame_silicon = 1.2
lame_germanium = 0.9
shear_silicon = 1.0
shear_germanium = 0.8
lame_medium = 1.05
shear_medium = 0.9
elastic_weight = 2.0
bond_energy = 0.7
base_rate = 1.0


def split(values):
    high = values.astype(ml_dtypes.bfloat16)
    return high, (values - high.astype(np.float64)).astype(ml_dtypes.bfloat16)


def waves(angle, axis):
    return np.concatenate([np.cos(angle), np.sin(angle)], axis)


def half_waves(angle):
    return np.concatenate([np.cos(angle[:144]), np.sin(angle[:128])], 0)


def tables():
    index = np.arange(256)
    angle = 2 * np.pi * (np.outer(index, index) % 256) / 256
    coarse = np.concatenate([index[:32], -index[:32] % 32])
    coarse = 2 * np.pi * (np.outer(coarse, index // 8) % 32) / 32
    order = np.concatenate([index[:129], 384 - index[129:]])
    both = np.concatenate([np.cos(angle[order]), np.sin(angle[order])], 1)
    back = np.concatenate([np.cos(angle[:, :128]), np.sin(angle[:, :128])], 1)
    back[:, 128] = np.cos(angle[:, 128])
    dft = split(half_waves(angle)) + split(waves(coarse, 0)) + split(back)
    lane = np.arange(128)
    turn_x = waves(2 * np.pi * np.outer(order, lane % 4) / POINTS, 0)
    turn_first = waves(2 * np.pi * np.outer(order, lane // 16 * 4 + lane % 4) / POINTS, 0)
    turn_y = waves(2 * np.pi * np.outer(np.arange(64) // 16, index) / POINTS, 0).reshape(2, 64, 256)
    stress = -2.0 * (lame_germanium + shear_germanium)
    angle = 2 * np.pi * np.outer(np.arange(16) // 4, np.arange(POINTS)) / POINTS
    turn_own = stress * np.stack([np.cos(angle), np.sin(angle)])
    turn_own = turn_own.reshape(2, 16, GY, COLS).transpose(2, 0, 1, 3)
    part, freq, comp, quad = lane // 64, lane // 16 % 4, lane // 4 % 4, lane % 4
    turns = np.outer(quad, quad) % 4
    cos4, sin4 = np.array([1, 0, -1, 0])[turns], np.array([0, 1, 0, -1])[turns]
    same_freq = freq[:, None] == freq[None, :]
    same_part = part[:, None] == part[None, :]
    to_real = part[None, :] == 0
    used = (comp[None, :] < 3) & same_freq
    forward = np.where(same_part, cos4, np.where(to_real, sin4, -sin4))
    forward4 = np.concatenate([forward * (used & (comp[:, None] == c)) for c in range(3)], 1)
    inverse = np.where(same_part, cos4, np.where(to_real, -sin4, sin4))
    inverse = inverse * (used & (comp[:, None] == comp[None, :]))
    turned = np.concatenate([-inverse[:, 64:], inverse[:, :64]], 1)
    inverse4 = np.concatenate([inverse, turned], 1)
    first4 = np.where((comp == 0)[:, None], forward4[:, :128], 0)
    picked = np.zeros((256, 128))
    for p in range(2):
        for n in range(128):
            picked[p * 128 + n] = first4[p * 64 + n // 4 % 4 * 16 + n % 4]
    both = np.concatenate(split(both), 0)
    small = np.concatenate([forward4, inverse4, picked[:128], picked[128:]], 1)
    return (
        np.concatenate(dft, 0),
        both,
        small.astype(ml_dtypes.bfloat16),
        np.concatenate([turn_x, turn_first], 0).reshape(4, 256, 128).astype(np.float32),
        turn_y.astype(np.float32),
        turn_own.astype(np.float32),
    )


def halves(values):
    high = values.astype(BF16)
    return high, (values - high.astype(F32)).astype(BF16)


def dot(left, right, dims):
    return lax.dot_general(left, right, (dims, ((), ())), preferred_element_type=F32)


def wide(table, values, dims):
    high, low = halves(values)
    both = dot(table[0][...], jnp.concatenate([high, low], 1 - dims[1][0]), dims)
    return both[:, :128] + both[:, 128:] + dot(table[1][...], high, dims)


def narrow(table, values, dims):
    return three([part[...] for part in table], halves(values), dims)


def parity(dft, multiply, plain, crossed, dims):
    even, odd = multiply(dft[0], plain, dims), multiply(dft[1], crossed, dims)
    minus = even[:128] - odd
    return jnp.concatenate(
        [even[:128] + odd, first_row(even[128:136], minus[:8]), minus[8:]], 0
    )


def first_row(special, others):
    return jnp.where(lax.broadcasted_iota(jnp.int32, others.shape, 0) == 0, special, others)


def folded(values):
    return values[:128] + values[128:], values[:128] - values[128:]


def three(left, right, dims):
    return dot(left[0], right[0], dims) + dot(left[0], right[1], dims) + dot(left[1], right[0], dims)


def exact(values, table):
    return dot(jnp.concatenate(halves(values), 1), jnp.concatenate([table, table], 0), ((1,), (0,)))


def green_tables(device, green):
    shape = (256, 128)
    lane = lax.broadcasted_iota(jnp.int32, shape, 1)
    comp = lax.rem(lane // 4, 4)
    row = lax.broadcasted_iota(jnp.int32, shape, 0)
    index_x = jnp.where(row > 128, 384 - row, row) + 256 * lax.rem(lane, 4)
    index_y = 4 * jnp.where(device > 128, 384 - device, device) + lax.rem(lane // 16, 4)
    unit = 2.0 * math.pi / POINTS
    a = jnp.where(index_x < POINTS // 2, index_x, index_x - POINTS).astype(F32) * unit
    b = jnp.where(index_y < POINTS // 2, index_y, index_y - POINTS).astype(F32) * unit
    ratio = (lame_medium + shear_medium) / (lame_medium + 2.0 * shear_medium)
    squared = a * a + b * b
    positive = squared > 0
    inverse_sq = jnp.where(positive, 1.0 / jnp.where(positive, squared, 1.0), 0.0)
    base = inverse_sq * (-1.0 / (shear_medium * POINTS * POINTS))
    edge_x = (index_x == POINTS // 2).astype(F32)
    edge_y = (index_y == POINTS // 2).astype(F32)
    odd = base * (1.0 - jnp.abs(edge_x - edge_y))
    aa, bb, ab = a * a, b * b, a * b
    xx_xx = (aa - ratio * aa * aa * inverse_sq) * base
    yy_yy = (bb - ratio * bb * bb * inverse_sq) * base
    xx_yy = -ratio * aa * bb * inverse_sq * base
    xx_xy = (ab - 2.0 * ratio * aa * ab * inverse_sq) * odd
    yy_xy = (ab - 2.0 * ratio * bb * ab * inverse_sq) * odd
    xy_xy = 0.5 * (aa + bb - 4.0 * ratio * aa * bb * inverse_sq) * base

    def pick(first, second, third):
        return jnp.where(
            comp == 0, first, jnp.where(comp == 1, second, jnp.where(comp == 2, third, 0.0))
        )

    green[0] = pick(xx_xx, xx_yy, 0.5 * xx_xy)
    green[1] = pick(xx_yy, yy_yy, 0.5 * yy_xy)
    green[2] = pick(xx_xy, yy_xy, xy_xy)


def crossing(shape):
    return jnp.where(lax.broadcasted_iota(jnp.int32, shape, 1) < 64, 1.0, -1.0)


def spectral(received, dft, back, turn, small, green):
    sign = crossing((256, 128))
    swapped = pltpu.roll(received, 64, 1) * sign
    first = wide(dft, jnp.concatenate([received, swapped], 0), ((1,), (0,)))
    turned = turn[0] * first + turn[1] * (pltpu.roll(first, 64, 1) * sign)
    spread = exact(turned, small[:, :384])
    mapped = (
        green[0] * spread[:, :128] + green[1] * spread[:, 128:256] + green[2] * spread[:, 256:]
    )
    return spectral_back(mapped, back, turn, small)


def spectral_back(mapped, back, turn, small):
    both = exact(mapped, small[:, 384:640])
    plain, crossed = both[:, :128], both[:, 128:]
    values = turn[0] * plain + turn[1] * crossed
    crossed = turn[0] * crossed - turn[1] * plain
    even, odd = folded(values)[0], folded(crossed)[1]
    even = [first_row(values[:8], even[:8]), even[8:]]
    odd = [first_row(values[128:136], odd[:8]), odd[8:]]
    return wide(back, jnp.concatenate(even + odd, 0), ((1,), (0,)))


def spectral_first(received, coarse, back, turn, small, green):
    both = three([part[...] for part in coarse], halves(received), ((1,), (0,)))
    cos, sin = both[:64], both[64:]
    real, imag = (
        jnp.concatenate([part[:32]] * 4 + [part[32:]] * 4, 0)
        for part in (cos[:, :128] + sin[:, 128:], cos[:, 128:] - sin[:, :128])
    )
    real, imag = turn[2] * real + turn[3] * imag, turn[2] * imag - turn[3] * real
    spread = exact(
        jnp.concatenate([real, imag], 1),
        jnp.concatenate([small[:, 640:768], small[:, 768:896]], 0),
    )
    return spectral_back((green[0] + green[1]) * spread, back, turn, small)


def first_y(fields, dft, turn, odd):
    upper = lax.broadcasted_iota(jnp.int32, (8, COLS), 0) < 4
    spread = []
    for field in fields:
        pieces = []
        for t in range(ROWS // 8):
            tile = field[8 * t : 8 * t + 8]
            other = pltpu.roll(tile, 4, 0)
            one, two = jnp.where(upper, tile, other), jnp.where(upper, other, tile)
            pieces += [one, one, two, two]
        spread.append(jnp.concatenate(pieces, 0))
    real, imag = spread
    cos, sin = (jnp.concatenate([turn[k]] * 8, 0) for k in range(2))
    real, imag = cos * real + sin * imag, cos * imag - sin * real
    plain, crossed = jnp.concatenate([real, imag], 0), jnp.concatenate([imag, -real], 0)
    table = [[part.at[:, pl.ds(0, 128)] for part in parts] for parts in dft]
    out = parity(table, narrow, plain, crossed, ((1,), (1,)))
    flip = lax.rem(lax.broadcasted_iota(jnp.int32, out.shape, 0), 2) * odd
    return out * (1 - 2 * flip).astype(F32)


def four(parts, sign):
    (r0, r1, r2, r3), (i0, i1, i2, i3) = parts
    er, ei, dr, di = r0 + r2, i0 + i2, r0 - r2, i0 - i2
    fr, fi, gr, gi = r1 + r3, i1 + i3, r1 - r3, i1 - i3
    up_r, up_i = dr - gi, di + gr
    down_r, down_i = dr + gi, di - gr
    if sign < 0:
        up_r, up_i, down_r, down_i = down_r, down_i, up_r, up_i
    return (er + fr, up_r, er - fr, down_r), (ei + fi, up_i, ei - fi, down_i)


def forward_y(stress, dft, turn_y):
    parts = [[field[:, 256 * a : 256 * a + 256] for a in range(4)] for field in stress]
    real, imag = (jnp.concatenate(list(part), 0) for part in four(parts, -1))
    turned_real = turn_y[0] * real + turn_y[1] * imag
    turned_imag = turn_y[0] * imag - turn_y[1] * real
    plain = jnp.concatenate([turned_real, turned_imag], 0)
    crossed = jnp.concatenate([turned_imag, -turned_real], 0)
    return parity(dft, wide, plain, crossed, ((1,), (1,)))


def inverse_y(received, back, turn_y):
    even, odd = folded(received)
    highest = pltpu.roll(received[128:136], 64, 1) * crossing((8, 128))
    even = [first_row(received[:8], even[:8]), even[8:]]
    odd = [first_row(highest, odd[:8]), odd[8:]]
    across = jnp.concatenate(even + odd, 0).T
    odd = jnp.concatenate([-across[64:, 128:], across[:64, 128:]], 0)
    rows = jnp.concatenate([across[:, :128], odd], 1)
    both = three(halves(rows), [part[...] for part in back], ((1,), (1,)))
    real, imag = both[:64], both[64:]
    turned_real = turn_y[0] * real - turn_y[1] * imag
    turned_imag = turn_y[0] * imag + turn_y[1] * real
    parts = [
        [part[16 * j : 16 * j + 16] for j in range(4)] for part in (turned_real, turned_imag)
    ]
    return [jnp.concatenate(list(part), 1) for part in four(parts, 1)]


def local_stress(normal, shear, fraction):
    lame_field = lame_silicon + (lame_germanium - lame_silicon) * fraction
    shear_field = 2.0 * (shear_silicon + (shear_germanium - shear_silicon) * fraction)
    excess = normal - fraction
    trace = excess + pltpu.roll(excess, 4, 0)
    return lame_field * trace + shear_field * excess, shear_field * shear, excess


def dft_parts(dfts):
    def rows(at, step, size):
        return [dfts.at[pl.ds(at + step * k, size)] for k in range(2)]

    return [rows(0, 272, 144), rows(144, 272, 128)], rows(544, 128, 128), rows(800, 256, 256)


def ring(steps, size):
    return min(steps % size, -steps % size)


def kernel(
    occupancy_in,
    colour_in,
    direction_in,
    barrier_in,
    dft_in,
    both_in,
    small_in,
    turn_in,
    turn_y_in,
    turn_own_in,
    strain_out,
    composition_out,
    occupancy,
    colour,
    direction,
    barrier,
    dfts,
    both,
    small,
    turn,
    turn_y,
    turn_own,
    green,
    normal,
    shear,
    fraction_pencil,
    first_sent,
    first_got,
    packed,
    landed,
    fraction_sent,
    fraction_got,
    static,
    rows_sent,
    rows_got,
    cols_sent,
    cols_got,
    corner_got,
    fields,
    strain_sent,
    strain_got,
    energy_sent,
    energy_got,
    input_sem,
    first_sem,
    send_sem,
    recv_sem,
    fraction_sem,
    halo_send,
    halo_recv,
    last_send,
    last_recv,
    edge_send,
    edge_recv,
):
    gx, gy = lax.axis_index("gx"), lax.axis_index("gy")
    me = gx * GY + gy
    z, core = lax.rem(gx // 2, 8), lax.rem(gx, 2)
    x, y = gy // 2, lax.rem(gy, 2) * 2 + gx // 16

    inputs = [
        (occupancy_in, occupancy),
        (dft_in, dfts),
        (turn_own_in.at[gy], turn_own),
        (barrier_in, barrier),
        (colour_in, colour),
        (direction_in, direction),
        (small_in, small),
        (turn_in, turn),
        (turn_y_in, turn_y),
        (both_in, both),
    ]
    inputs = [
        pltpu.make_async_copy(source, target, input_sem.at[k])
        for k, (source, target) in enumerate(inputs)
    ]
    x_part = [lax.rem(x + dx, 4) * 2 for dx in range(4)]
    y_part = [lax.rem(y + dy, 4) for dy in range(4)]
    y_part = [(lax.rem(there, 2) * 16, there // 2) for there in y_part]
    c_part = [core, 1 - core]
    groups = [[] for _ in range(5)]
    for dx in range(4):
        for dy in range(4):
            for dc in (1, 0):
                there = (y_part[dy][0] + c_part[dc], x_part[dx] + y_part[dy][1])
                groups[ring(dx, 4) + ring(dy, 4)].append(there)

    def to_others(send):
        def at(z_there, places):
            for gx_part, gy_there in places:
                send(gx_part + 2 * z_there, gy_there)

        def step(i, carry):
            for hops in (4, 3, 2, 1, 0):
                along_z = 8 - i - hops
                up_z, down_z = lax.rem(z + along_z + 8, 8), lax.rem(z - along_z + 8, 8)
                within = (along_z >= 0) & (along_z <= 4)
                if hops > 0:
                    pl.when(within)(functools.partial(at, up_z, groups[hops]))
                else:
                    pl.when(within)(functools.partial(at, up_z, groups[0][:1]))
                    pl.when((along_z >= 1) & within)(functools.partial(at, up_z, groups[0][1:]))
                pl.when((along_z >= 1) & (along_z <= 3))(
                    functools.partial(at, down_z, groups[hops])
                )
            return carry

        lax.fori_loop(0, 9, step, 0)

    entry = pltpu.get_barrier_semaphore()
    flat = [place for hops in (4, 3, 2, 1, 0) for place in groups[hops]]
    flat = flat[:-2] + [groups[0][0], groups[0][1]]

    def greet(z_there, places):
        for gx_part, gy_there in places:
            pl.semaphore_signal(
                entry, inc=1, device_id=(gx_part + 2 * z_there, gy_there), device_id_type=MESH
            )

    def greet_step(i, carry):
        steps = jnp.where(lax.rem(i, 2) == 0, 4 + i // 2, 4 - (i + 1) // 2)
        greet(lax.rem(z + steps, 8), flat)
        return carry

    lax.fori_loop(0, 7, greet_step, 0)
    greet(z, flat[:-1])

    for copy in inputs:
        copy.start()

    dft, coarse, back = dft_parts(dfts)
    whole = [both.at[pl.ds(256 * k, 256)] for k in range(2)]

    for copy in inputs[:3]:
        copy.wait()
    for layer in range(2):
        static[layer] = occupancy[layer].astype(F32)
    rows = first_y([static[0], static[1]], dft, turn_own, lax.rem(gy, 2))
    first_sent[:, 0, :] = rows[:, :128]
    first_sent[:, 1, :] = rows[:, 128:]
    first_got[me] = first_sent[me]
    for there in range(GY):
        part = slice(4 * there, 4 * there + 4)
        fraction_sent[there] = jnp.concatenate([static[0, part], static[1, part]], 0)
    fraction_got[gy] = fraction_sent[gy]

    pl.semaphore_wait(entry, DEVICES - 1)

    def send_first(there_x, there_y):
        pltpu.make_async_remote_copy(
            first_sent.at[there_x * GY + there_y],
            first_got.at[me],
            first_sem.at[0],
            first_sem.at[1],
            device_id=(there_x, there_y),
            device_id_type=MESH,
        ).start()

    to_others(send_first)

    def total(source, target, send, recv, rows):
        return pltpu.make_async_remote_copy(
            source.at[pl.ds(0, rows)],
            target.at[pl.ds(0, rows)],
            send,
            recv,
            device_id=(gx + 1 - 2 * core, gy),
            device_id_type=MESH,
        )

    offsets = sorted(
        [(dx, dy) for dx in range(4) for dy in range(2) if dx + dy > 0],
        key=lambda t: -(ring(t[0], 4) + 2 * t[1]),
    )
    peers = [lax.rem(x + dx, 4) * 2 + lax.rem(gy + dy, 2) for dx, dy in offsets]

    def to_peers(source, target, send, recv):
        for there in peers:
            pltpu.make_async_remote_copy(
                source.at[there],
                target.at[gy],
                send,
                recv,
                device_id=(gx, there),
                device_id_type=MESH,
            ).start()
        return total(source, target, send, recv, GY - 1)

    fraction_copies = to_peers(fraction_sent, fraction_got, fraction_sem.at[0], fraction_sem.at[1])

    for copy in inputs[3:]:
        copy.wait()
    for layer in range(2):
        static[2 + layer] = barrier[layer]
        static[4 + layer] = colour[layer].astype(F32)
        for section in range(SECTIONS):
            static[6 + 2 * section + layer] = direction[section, layer].astype(F32)
    upper = lax.broadcasted_iota(jnp.int32, (8, COLS), 0) < 4
    for kind in range(STATIC // 2):
        one, two = static[2 * kind], static[2 * kind + 1]
        rows_sent[0, kind] = jnp.where(upper, one[:8], pltpu.roll(two[:8], 4, 0))
        rows_sent[1, kind] = jnp.where(upper, pltpu.roll(one[-8:], 4, 0), two[-8:])
    flat = [static[k] for k in range(STATIC)] + [jnp.zeros((64, COLS), F32)]
    across = jnp.concatenate(flat, 0).T
    cols_sent[0] = across[:8]
    cols_sent[1] = across[-8:]

    up, down = lax.rem(gx + 1, GX), lax.rem(gx + GX - 1, GX)
    after, before = lax.rem(gy + 1, GY), lax.rem(gy + GY - 1, GY)
    halos = [
        (rows_sent.at[0], rows_got.at[0], (down, gy)),
        (rows_sent.at[1], rows_got.at[1], (up, gy)),
        (cols_sent.at[0], cols_got.at[0], (gx, before)),
        (cols_sent.at[1], cols_got.at[1], (gx, after)),
        (cols_sent.at[0], corner_got.at[0], (down, before)),
        (cols_sent.at[1], corner_got.at[1], (down, after)),
        (cols_sent.at[0], corner_got.at[2], (up, before)),
        (cols_sent.at[1], corner_got.at[3], (up, after)),
    ]
    halos = [
        pltpu.make_async_remote_copy(
            source, target, halo_send.at[k], halo_recv.at[k], device_id=there, device_id_type=MESH
        )
        for k, (source, target, there) in enumerate(halos)
    ]
    for copy in halos:
        copy.start()
    green_tables(me, green)

    total(first_sent, first_got, first_sem.at[0], first_sem.at[1], DEVICES - 1).wait_recv()
    received = jnp.concatenate([first_got[:, 0, :], first_got[:, 1, :]], 1)

    def start_exchange(slot, rows):
        packed[slot, :, 0, :] = rows

        def send(there_x, there_y):
            pltpu.make_async_remote_copy(
                packed.at[slot, there_x * GY + there_y],
                landed.at[slot, me],
                send_sem.at[slot],
                recv_sem.at[slot],
                device_id=(there_x, there_y),
                device_id_type=MESH,
            ).start()

        to_others(send)
        landed[slot, me] = packed[slot, me]

    def exchanged(slot):
        return total(
            packed.at[slot], landed.at[slot], send_sem.at[slot], recv_sem.at[slot], DEVICES - 1
        )

    def end_exchange(slot):
        exchanged(slot).wait_recv()
        return landed[slot, :, 0, :]

    start_exchange(0, spectral_first(received, coarse, back, turn, small, green))

    fraction_copies.wait_recv()
    pencil = jnp.concatenate([fraction_got[g] for g in range(GY)], 1)
    other = pltpu.roll(pencil, 4, 0)
    upper_wide = lax.broadcasted_iota(jnp.int32, (8, POINTS), 0) < 4
    fraction_pencil[0] = jnp.where(upper_wide, pencil, other)
    fraction_pencil[1] = jnp.where(upper_wide, other, pencil)
    for copy in halos:
        copy.wait_recv()

    def side(ahead, behind):
        gap = jnp.zeros((COLS - 16, 384), F32)
        return jnp.concatenate([ahead, gap, behind], 0).T

    beside = side(cols_got[0], cols_got[1])
    below = side(corner_got[0], corner_got[1])
    above = side(corner_got[2], corner_got[3])
    for k in range(STATIC):
        kind, layer = k // 2, k % 2
        part = slice(ROWS * k, ROWS * k + ROWS)
        fields[k, :ROWS, :COLS] = static[k]
        fields[k, :ROWS, COLS:] = beside[part]
        low, high = rows_got[0, kind], rows_got[1, kind]
        if layer == 0:
            high = pltpu.roll(high, 4, 0)
        else:
            low = pltpu.roll(low, 4, 0)
        fields[k, ROWS:, :COLS] = jnp.where(upper, low, high)
        fields[k, ROWS:, COLS:] = jnp.where(upper, below[part][:8], above[part][-8:])

    change = inverse_y(end_exchange(0), back, turn_y)
    for p in range(2):
        normal[p] = change[p][:8]
        shear[p] = change[p][8:]

    def sweep(i, carry):
        stress = []
        for p in range(2):
            stress_normal, stress_shear, _ = local_stress(normal[p], shear[p], fraction_pencil[p])
            stress.append(jnp.concatenate([stress_normal, stress_shear], 0))
        start_exchange(2 * i + 1, forward_y(stress, dft, turn_y))
        arrived = end_exchange(2 * i + 1)
        start_exchange(2 * i + 2, spectral(arrived, whole, back, turn, small, green))
        change = inverse_y(end_exchange(2 * i + 2), back, turn_y)
        for p in range(2):
            normal[p] += change[p][:8]
            shear[p] += change[p][8:]
        return carry

    lax.fori_loop(0, ITERS - 1, sweep, 0)

    energies = []
    for p in range(2):
        stress_normal, stress_shear, excess = local_stress(normal[p], shear[p], fraction_pencil[p])
        density = stress_normal * excess + 2.0 * stress_shear * shear[p]
        energies.append(0.5 * (density + pltpu.roll(density, 4, 0)))
    energy = jnp.where(upper_wide, energies[0], energies[1])
    shears = jnp.where(upper_wide, shear[0], pltpu.roll(shear[1], 4, 0))
    left = lax.broadcasted_iota(jnp.int32, (8, COLS), 1) < COLS // 2

    def block(values, g):
        return values[:, COLS * (g % GY) : COLS * (g % GY) + COLS]

    for g in range(GY):
        energy_sent[g, :, :COLS] = block(energy, g)
        energy_sent[g, :, COLS:] = jnp.where(left, block(energy, g + 1), block(energy, g - 1))

    def edge_copy(g, slot, there):
        return pltpu.make_async_remote_copy(
            energy_sent.at[g],
            energy_got.at[GY + slot],
            edge_send.at[slot],
            edge_recv.at[slot],
            device_id=(there, g),
            device_id_type=MESH,
        )

    @pl.when(gy == 0)
    def _():
        for g in range(GY):
            edge_copy(g, 0, down).start()

    @pl.when(gy == GY - 1)
    def _():
        for g in range(GY):
            edge_copy(g, 1, up).start()

    energy_copies = to_peers(energy_sent, energy_got, last_send.at[0], last_recv.at[0])
    for g in range(GY):
        strain_sent[g, 0:8] = block(normal[0], g)
        strain_sent[g, 8:16] = block(normal[1], g)
        strain_sent[g, 16:24] = block(shears, g)
    strain_copies = to_peers(strain_sent, strain_got, last_send.at[1], last_recv.at[1])
    energy_got[gy] = energy_sent[gy]
    strain_got[gy] = strain_sent[gy]

    total(first_sent, first_got, first_sem.at[0], first_sem.at[1], DEVICES - 1).wait_send()
    fraction_copies.wait_send()
    for copy in halos:
        copy.wait_send()
    for slot in range(2 * ITERS - 1):
        exchanged(slot).wait_send()

    low = lax.broadcasted_iota(jnp.int32, (8, 2 * COLS), 0) < 4
    tall, wide_cols = ROWS + 8, 2 * COLS

    def prepared(sites, layer, section):
        way = fields[6 + 2 * section + layer]
        above, below = pltpu.roll(sites, 1, 0), pltpu.roll(sites, tall - 1, 0)
        ahead, behind = pltpu.roll(sites, wide_cols - 1, 1), pltpu.roll(sites, 1, 1)
        neighbours = above + below + behind + ahead
        target = jnp.where(
            way == 0.0,
            below,
            jnp.where(way == 1.0, above, jnp.where(way == 2.0, ahead, behind)),
        )
        moving = jnp.where(
            fields[4 + layer] == float(section), sites * (1.0 - target), 0.0
        )
        return bond_energy * neighbours - (fields[2 + layer] + base_rate), moving

    def hop(sites, ready, energy, layer, section):
        flux = ready[1] / (1.0 + jnp.exp(ready[0] - elastic_weight * energy))
        way = fields[6 + 2 * section + layer]
        parted = [jnp.where(way == float(number), flux, 0.0) for number in range(4)]
        return (
            sites
            - flux
            + (
                pltpu.roll(parted[0], 1, 0)
                + pltpu.roll(parted[1], tall - 1, 0)
                + pltpu.roll(parted[2], 1, 1)
                + pltpu.roll(parted[3], wide_cols - 1, 1)
            )
        )

    ready = [prepared(fields[layer], layer, 0) for layer in range(2)]

    energy_copies.wait_recv()
    for slot in range(2):
        edge_copy(0, slot, up).wait_recv()

    for layer in range(2):
        pieces = []
        for pair in range(GY // 2 + 1):
            one, two = energy_got[2 * pair], energy_got[2 * pair + 1]
            if layer == 0:
                pieces.append(jnp.where(low, one, pltpu.roll(two, 4, 0)))
            else:
                pieces.append(jnp.where(low, pltpu.roll(one, 4, 0), two))
        energy_here = jnp.concatenate(pieces, 0)
        sites = hop(fields[layer], ready[layer], energy_here, layer, 0)
        for section in range(1, SECTIONS):
            sites = hop(sites, prepared(sites, layer, section), energy_here, layer, section)
        composition_out[layer] = sites[:ROWS, :COLS]

    strain_copies.wait_recv()
    for g in range(GY):
        rows = slice(4 * g, 4 * g + 4)
        for layer in range(2):
            strain_out[0, layer, rows] = strain_got[g, 8 * layer : 8 * layer + 4]
            strain_out[1, layer, rows] = strain_got[g, 8 * layer + 4 : 8 * layer + 8]
            strain_out[2, layer, rows] = strain_got[g, 16 + 4 * layer : 20 + 4 * layer]

    energy_copies.wait_send()
    strain_copies.wait_send()

    @pl.when(gy == 0)
    def _():
        for g in range(GY):
            edge_copy(g, 0, down).wait_send()

    @pl.when(gy == GY - 1)
    def _():
        for g in range(GY):
            edge_copy(g, 1, up).wait_send()


def on_device(occupancy, colour, hop_direction, barrier):
    operands = (occupancy, colour, hop_direction, barrier) + tuple(
        jnp.asarray(table) for table in tables()
    )
    vmem = pl.BlockSpec(memory_space=pltpu.VMEM)
    dma = pltpu.SemaphoreType.DMA
    exchanges = 2 * ITERS - 1
    return pl.pallas_call(
        kernel,
        out_shape=(
            jax.ShapeDtypeStruct((3, 2, ROWS, COLS), F32),
            jax.ShapeDtypeStruct((2, ROWS, COLS), F32),
        ),
        in_specs=[pl.BlockSpec(memory_space=pltpu.HBM)] * len(operands),
        out_specs=(vmem, vmem),
        scratch_shapes=[
            pltpu.VMEM((2, ROWS, COLS), jnp.int32),
            pltpu.VMEM((2, ROWS, COLS), jnp.int32),
            pltpu.VMEM((2, 2, ROWS, COLS), jnp.int32),
            pltpu.VMEM((2, ROWS, COLS), F32),
            pltpu.VMEM((1312, 256), BF16),
            pltpu.VMEM((512, 512), BF16),
            pltpu.VMEM((128, 896), BF16),
            pltpu.VMEM((4, 256, 128), F32),
            pltpu.VMEM((2, 64, 256), F32),
            pltpu.VMEM((2, 16, COLS), F32),
            pltpu.VMEM((3, 256, 128), F32),
            pltpu.VMEM((2, 8, POINTS), F32),
            pltpu.VMEM((2, 8, POINTS), F32),
            pltpu.VMEM((2, 8, POINTS), F32),
            pltpu.VMEM((DEVICES, 2, 128), F32),
            pltpu.VMEM((DEVICES, 2, 128), F32),
            pltpu.VMEM((exchanges, DEVICES, 1, 128), F32),
            pltpu.VMEM((exchanges, DEVICES, 1, 128), F32),
            pltpu.VMEM((GY, 8, COLS), F32),
            pltpu.VMEM((GY, 8, COLS), F32),
            pltpu.VMEM((STATIC, ROWS, COLS), F32),
            pltpu.VMEM((2, STATIC // 2, 8, COLS), F32),
            pltpu.VMEM((2, STATIC // 2, 8, COLS), F32),
            pltpu.VMEM((2, 8, 384), F32),
            pltpu.VMEM((2, 8, 384), F32),
            pltpu.VMEM((4, 8, 384), F32),
            pltpu.VMEM((STATIC, ROWS + 8, 2 * COLS), F32),
            pltpu.VMEM((GY, 24, COLS), F32),
            pltpu.VMEM((GY, 24, COLS), F32),
            pltpu.VMEM((GY, 8, 2 * COLS), F32),
            pltpu.VMEM((GY + 2, 8, 2 * COLS), F32),
            dma((10,)),
            dma((2,)),
            dma((exchanges,)),
            dma((exchanges,)),
            dma((2,)),
            dma((8,)),
            dma((8,)),
            dma((2,)),
            dma((2,)),
            dma((2,)),
            dma((2,)),
        ],
        compiler_params=pltpu.CompilerParams(
            collective_id=0, has_side_effects=True, vmem_limit_bytes=40 * 1024 * 1024
        ),
        name="film",
    )(*[pltpu.with_memory_space_constraint(x, pltpu.HBM) for x in operands])


def solution(mesh):
    placed = (
        P(None, "gx", "gy"),
        P(None, "gx", "gy"),
        P(None, None, "gx", "gy"),
        P(None, "gx", "gy"),
    )
    return jax.shard_map(
        on_device,
        mesh=mesh,
        in_specs=placed,
        out_specs=(P(None, None, "gx", "gy"), P(None, "gx", "gy")),
        check_vma=False,
    )
```

```python
import functools
import math

import jax
import jax.numpy as jnp
import ml_dtypes
import numpy as np
from jax import lax
from jax.experimental import pallas as pl
from jax.experimental.pallas import tpu as pltpu
from jax.sharding import PartitionSpec as P

MESH = pl.DeviceIdType.MESH
F32 = jnp.float32
BF16 = jnp.bfloat16

ITERS = 3
SECTIONS = 2
GX, GY = 32, 8
DEVICES = GX * GY
POINTS = 1024
ROWS, COLS = POINTS // GX, POINTS // GY
STATIC = 10

lame_silicon = 1.2
lame_germanium = 0.9
shear_silicon = 1.0
shear_germanium = 0.8
lame_medium = 1.05
shear_medium = 0.9
elastic_weight = 2.0
bond_energy = 0.7
base_rate = 1.0


def split(values):
    high = values.astype(ml_dtypes.bfloat16)
    return high, (values - high.astype(np.float64)).astype(ml_dtypes.bfloat16)


def waves(angle, axis):
    return np.concatenate([np.cos(angle), np.sin(angle)], axis)


def half_waves(angle):
    return np.concatenate([np.cos(angle[:144]), np.sin(angle[:128])], 0)


def tables():
    index = np.arange(256)
    angle = 2 * np.pi * (np.outer(index, index) % 256) / 256
    coarse = np.concatenate([index[:32], -index[:32] % 32])
    coarse = 2 * np.pi * (np.outer(coarse, index // 8) % 32) / 32
    order = np.concatenate([index[:129], 384 - index[129:]])
    both = np.concatenate([np.cos(angle[order]), np.sin(angle[order])], 1)
    back = np.concatenate([np.cos(angle[:, :128]), np.sin(angle[:, :128])], 1)
    back[:, 128] = np.cos(angle[:, 128])
    dft = split(half_waves(angle)) + split(waves(coarse, 0)) + split(back)
    lane = np.arange(128)
    turn_x = waves(2 * np.pi * np.outer(order, lane % 4) / POINTS, 0)
    turn_first = waves(2 * np.pi * np.outer(order, lane // 16 * 4 + lane % 4) / POINTS, 0)
    turn_y = waves(2 * np.pi * np.outer(np.arange(64) // 16, index) / POINTS, 0).reshape(2, 64, 256)
    stress = -2.0 * (lame_germanium + shear_germanium)
    angle = 2 * np.pi * np.outer(np.arange(16) // 4, np.arange(POINTS)) / POINTS
    turn_own = stress * np.stack([np.cos(angle), np.sin(angle)])
    turn_own = turn_own.reshape(2, 16, GY, COLS).transpose(2, 0, 1, 3)
    part, freq, comp, quad = lane // 64, lane // 16 % 4, lane // 4 % 4, lane % 4
    turns = np.outer(quad, quad) % 4
    cos4, sin4 = np.array([1, 0, -1, 0])[turns], np.array([0, 1, 0, -1])[turns]
    same_freq = freq[:, None] == freq[None, :]
    same_part = part[:, None] == part[None, :]
    to_real = part[None, :] == 0
    used = (comp[None, :] < 3) & same_freq
    forward = np.where(same_part, cos4, np.where(to_real, sin4, -sin4))
    forward4 = np.concatenate([forward * (used & (comp[:, None] == c)) for c in range(3)], 1)
    inverse = np.where(same_part, cos4, np.where(to_real, -sin4, sin4))
    inverse = inverse * (used & (comp[:, None] == comp[None, :]))
    turned = np.concatenate([-inverse[:, 64:], inverse[:, :64]], 1)
    inverse4 = np.concatenate([inverse, turned], 1)
    first4 = np.where((comp == 0)[:, None], forward4[:, :128], 0)
    picked = np.zeros((256, 128))
    for p in range(2):
        for n in range(128):
            picked[p * 128 + n] = first4[p * 64 + n // 4 % 4 * 16 + n % 4]
    both = np.concatenate(split(both), 0)
    small = np.concatenate([forward4, inverse4, picked[:128], picked[128:]], 1)
    return (
        np.concatenate(dft, 0),
        both,
        small.astype(ml_dtypes.bfloat16),
        np.concatenate([turn_x, turn_first], 0).reshape(4, 256, 128).astype(np.float32),
        turn_y.astype(np.float32),
        turn_own.astype(np.float32),
    )


def halves(values):
    high = values.astype(BF16)
    return high, (values - high.astype(F32)).astype(BF16)


def dot(left, right, dims):
    return lax.dot_general(left, right, (dims, ((), ())), preferred_element_type=F32)


def wide(table, values, dims):
    high, low = halves(values)
    both = dot(table[0][...], jnp.concatenate([high, low], 1 - dims[1][0]), dims)
    return both[:, :128] + both[:, 128:] + dot(table[1][...], high, dims)


def narrow(table, values, dims):
    return three([part[...] for part in table], halves(values), dims)


def parity(dft, multiply, plain, crossed, dims):
    even, odd = multiply(dft[0], plain, dims), multiply(dft[1], crossed, dims)
    minus = even[:128] - odd
    return jnp.concatenate(
        [even[:128] + odd, first_row(even[128:136], minus[:8]), minus[8:]], 0
    )


def first_row(special, others):
    return jnp.where(lax.broadcasted_iota(jnp.int32, others.shape, 0) == 0, special, others)


def folded(values):
    return values[:128] + values[128:], values[:128] - values[128:]


def three(left, right, dims):
    return dot(left[0], right[0], dims) + dot(left[0], right[1], dims) + dot(left[1], right[0], dims)


def exact(values, table):
    return dot(jnp.concatenate(halves(values), 1), jnp.concatenate([table, table], 0), ((1,), (0,)))


def green_tables(device, green):
    shape = (256, 128)
    lane = lax.broadcasted_iota(jnp.int32, shape, 1)
    comp = lax.rem(lane // 4, 4)
    row = lax.broadcasted_iota(jnp.int32, shape, 0)
    index_x = jnp.where(row > 128, 384 - row, row) + 256 * lax.rem(lane, 4)
    index_y = 4 * jnp.where(device > 128, 384 - device, device) + lax.rem(lane // 16, 4)
    unit = 2.0 * math.pi / POINTS
    a = jnp.where(index_x < POINTS // 2, index_x, index_x - POINTS).astype(F32) * unit
    b = jnp.where(index_y < POINTS // 2, index_y, index_y - POINTS).astype(F32) * unit
    ratio = (lame_medium + shear_medium) / (lame_medium + 2.0 * shear_medium)
    squared = a * a + b * b
    positive = squared > 0
    inverse_sq = jnp.where(positive, 1.0 / jnp.where(positive, squared, 1.0), 0.0)
    base = inverse_sq * (-1.0 / (shear_medium * POINTS * POINTS))
    edge_x = (index_x == POINTS // 2).astype(F32)
    edge_y = (index_y == POINTS // 2).astype(F32)
    odd = base * (1.0 - jnp.abs(edge_x - edge_y))
    aa, bb, ab = a * a, b * b, a * b
    xx_xx = (aa - ratio * aa * aa * inverse_sq) * base
    yy_yy = (bb - ratio * bb * bb * inverse_sq) * base
    xx_yy = -ratio * aa * bb * inverse_sq * base
    xx_xy = (ab - 2.0 * ratio * aa * ab * inverse_sq) * odd
    yy_xy = (ab - 2.0 * ratio * bb * ab * inverse_sq) * odd
    xy_xy = 0.5 * (aa + bb - 4.0 * ratio * aa * bb * inverse_sq) * base

    def pick(first, second, third):
        return jnp.where(
            comp == 0, first, jnp.where(comp == 1, second, jnp.where(comp == 2, third, 0.0))
        )

    green[0] = pick(xx_xx, xx_yy, 0.5 * xx_xy)
    green[1] = pick(xx_yy, yy_yy, 0.5 * yy_xy)
    green[2] = pick(xx_xy, yy_xy, xy_xy)


def crossing(shape):
    return jnp.where(lax.broadcasted_iota(jnp.int32, shape, 1) < 64, 1.0, -1.0)


def spectral(received, dft, back, turn, small, green):
    sign = crossing((256, 128))
    swapped = pltpu.roll(received, 64, 1) * sign
    first = wide(dft, jnp.concatenate([received, swapped], 0), ((1,), (0,)))
    turned = turn[0] * first + turn[1] * (pltpu.roll(first, 64, 1) * sign)
    spread = exact(turned, small[:, :384])
    mapped = (
        green[0] * spread[:, :128] + green[1] * spread[:, 128:256] + green[2] * spread[:, 256:]
    )
    return spectral_back(mapped, back, turn, small)


def spectral_back(mapped, back, turn, small):
    both = exact(mapped, small[:, 384:640])
    plain, crossed = both[:, :128], both[:, 128:]
    values = turn[0] * plain + turn[1] * crossed
    crossed = turn[0] * crossed - turn[1] * plain
    even, odd = folded(values)[0], folded(crossed)[1]
    even = [first_row(values[:8], even[:8]), even[8:]]
    odd = [first_row(values[128:136], odd[:8]), odd[8:]]
    return wide(back, jnp.concatenate(even + odd, 0), ((1,), (0,)))


def spectral_first(received, coarse, back, turn, small, green):
    both = three([part[...] for part in coarse], halves(received), ((1,), (0,)))
    cos, sin = both[:64], both[64:]
    real, imag = (
        jnp.concatenate([part[:32]] * 4 + [part[32:]] * 4, 0)
        for part in (cos[:, :128] + sin[:, 128:], cos[:, 128:] - sin[:, :128])
    )
    real, imag = turn[2] * real + turn[3] * imag, turn[2] * imag - turn[3] * real
    spread = exact(
        jnp.concatenate([real, imag], 1),
        jnp.concatenate([small[:, 640:768], small[:, 768:896]], 0),
    )
    return spectral_back((green[0] + green[1]) * spread, back, turn, small)


def first_y(fields, dft, turn, odd):
    upper = lax.broadcasted_iota(jnp.int32, (8, COLS), 0) < 4
    spread = []
    for field in fields:
        pieces = []
        for t in range(ROWS // 8):
            tile = field[8 * t : 8 * t + 8]
            other = pltpu.roll(tile, 4, 0)
            one, two = jnp.where(upper, tile, other), jnp.where(upper, other, tile)
            pieces += [one, one, two, two]
        spread.append(jnp.concatenate(pieces, 0))
    real, imag = spread
    cos, sin = (jnp.concatenate([turn[k]] * 8, 0) for k in range(2))
    real, imag = cos * real + sin * imag, cos * imag - sin * real
    plain, crossed = jnp.concatenate([real, imag], 0), jnp.concatenate([imag, -real], 0)
    table = [[part.at[:, pl.ds(0, 128)] for part in parts] for parts in dft]
    out = parity(table, narrow, plain, crossed, ((1,), (1,)))
    flip = lax.rem(lax.broadcasted_iota(jnp.int32, out.shape, 0), 2) * odd
    return out * (1 - 2 * flip).astype(F32)


def four(parts, sign):
    (r0, r1, r2, r3), (i0, i1, i2, i3) = parts
    er, ei, dr, di = r0 + r2, i0 + i2, r0 - r2, i0 - i2
    fr, fi, gr, gi = r1 + r3, i1 + i3, r1 - r3, i1 - i3
    up_r, up_i = dr - gi, di + gr
    down_r, down_i = dr + gi, di - gr
    if sign < 0:
        up_r, up_i, down_r, down_i = down_r, down_i, up_r, up_i
    return (er + fr, up_r, er - fr, down_r), (ei + fi, up_i, ei - fi, down_i)


def forward_y(stress, dft, turn_y):
    parts = [[field[:, 256 * a : 256 * a + 256] for a in range(4)] for field in stress]
    real, imag = (jnp.concatenate(list(part), 0) for part in four(parts, -1))
    turned_real = turn_y[0] * real + turn_y[1] * imag
    turned_imag = turn_y[0] * imag - turn_y[1] * real
    plain = jnp.concatenate([turned_real, turned_imag], 0)
    crossed = jnp.concatenate([turned_imag, -turned_real], 0)
    return parity(dft, wide, plain, crossed, ((1,), (1,)))


def inverse_y(received, back, turn_y):
    even, odd = folded(received)
    highest = pltpu.roll(received[128:136], 64, 1) * crossing((8, 128))
    even = [first_row(received[:8], even[:8]), even[8:]]
    odd = [first_row(highest, odd[:8]), odd[8:]]
    across = jnp.concatenate(even + odd, 0).T
    odd = jnp.concatenate([-across[64:, 128:], across[:64, 128:]], 0)
    rows = jnp.concatenate([across[:, :128], odd], 1)
    both = three(halves(rows), [part[...] for part in back], ((1,), (1,)))
    real, imag = both[:64], both[64:]
    turned_real = turn_y[0] * real - turn_y[1] * imag
    turned_imag = turn_y[0] * imag + turn_y[1] * real
    parts = [
        [part[16 * j : 16 * j + 16] for j in range(4)] for part in (turned_real, turned_imag)
    ]
    return [jnp.concatenate(list(part), 1) for part in four(parts, 1)]


def local_stress(normal, shear, fraction):
    lame_field = lame_silicon + (lame_germanium - lame_silicon) * fraction
    shear_field = 2.0 * (shear_silicon + (shear_germanium - shear_silicon) * fraction)
    excess = normal - fraction
    trace = excess + pltpu.roll(excess, 4, 0)
    return lame_field * trace + shear_field * excess, shear_field * shear, excess


def dft_parts(dfts):
    def rows(at, step, size):
        return [dfts.at[pl.ds(at + step * k, size)] for k in range(2)]

    return [rows(0, 272, 144), rows(144, 272, 128)], rows(544, 128, 128), rows(800, 256, 256)


def ring(steps, size):
    return min(steps % size, -steps % size)


def kernel(
    occupancy_in,
    colour_in,
    direction_in,
    barrier_in,
    dft_in,
    both_in,
    small_in,
    turn_in,
    turn_y_in,
    turn_own_in,
    strain_out,
    composition_out,
    occupancy,
    colour,
    direction,
    barrier,
    dfts,
    both,
    small,
    turn,
    turn_y,
    turn_own,
    green,
    normal,
    shear,
    fraction_pencil,
    first_sent,
    first_got,
    packed,
    landed,
    fraction_sent,
    fraction_got,
    static,
    rows_sent,
    rows_got,
    cols_sent,
    cols_got,
    corner_got,
    fields,
    strain_sent,
    strain_got,
    energy_sent,
    energy_got,
    input_sem,
    first_sem,
    send_sem,
    recv_sem,
    fraction_sem,
    halo_send,
    halo_recv,
    last_send,
    last_recv,
    edge_send,
    edge_recv,
):
    gx, gy = lax.axis_index("gx"), lax.axis_index("gy")
    me = gx * GY + gy
    z, core = lax.rem(gx // 2, 8), lax.rem(gx, 2)
    x, y = gy // 2, lax.rem(gy, 2) * 2 + gx // 16

    inputs = [
        (occupancy_in, occupancy),
        (dft_in, dfts),
        (turn_own_in.at[gy], turn_own),
        (barrier_in, barrier),
        (colour_in, colour),
        (direction_in, direction),
        (small_in, small),
        (turn_in, turn),
        (turn_y_in, turn_y),
        (both_in, both),
    ]
    inputs = [
        pltpu.make_async_copy(source, target, input_sem.at[k])
        for k, (source, target) in enumerate(inputs)
    ]
    x_part = [lax.rem(x + dx, 4) * 2 for dx in range(4)]
    y_part = [lax.rem(y + dy, 4) for dy in range(4)]
    y_part = [(lax.rem(there, 2) * 16, there // 2) for there in y_part]
    c_part = [core, 1 - core]
    groups = [[] for _ in range(5)]
    for dx in range(4):
        for dy in range(4):
            for dc in (1, 0):
                there = (y_part[dy][0] + c_part[dc], x_part[dx] + y_part[dy][1])
                groups[ring(dx, 4) + ring(dy, 4)].append(there)

    def to_others(send):
        def at(z_there, places):
            for gx_part, gy_there in places:
                send(gx_part + 2 * z_there, gy_there)

        def step(i, carry):
            for hops in (4, 3, 2, 1, 0):
                along_z = 8 - i - hops
                up_z, down_z = lax.rem(z + along_z + 8, 8), lax.rem(z - along_z + 8, 8)
                within = (along_z >= 0) & (along_z <= 4)
                if hops > 0:
                    pl.when(within)(functools.partial(at, up_z, groups[hops]))
                else:
                    pl.when(within)(functools.partial(at, up_z, groups[0][:1]))
                    pl.when((along_z >= 1) & within)(functools.partial(at, up_z, groups[0][1:]))
                pl.when((along_z >= 1) & (along_z <= 3))(
                    functools.partial(at, down_z, groups[hops])
                )
            return carry

        lax.fori_loop(0, 9, step, 0)

    entry = pltpu.get_barrier_semaphore()
    to_others(
        lambda there_x, there_y: pl.semaphore_signal(
            entry, inc=1, device_id=(there_x, there_y), device_id_type=MESH
        )
    )

    for copy in inputs:
        copy.start()

    dft, coarse, back = dft_parts(dfts)
    whole = [both.at[pl.ds(256 * k, 256)] for k in range(2)]

    for copy in inputs[:3]:
        copy.wait()
    for layer in range(2):
        static[layer] = occupancy[layer].astype(F32)
    rows = first_y([static[0], static[1]], dft, turn_own, lax.rem(gy, 2))
    first_sent[:, 0, :] = rows[:, :128]
    first_sent[:, 1, :] = rows[:, 128:]
    first_got[me] = first_sent[me]
    for there in range(GY):
        part = slice(4 * there, 4 * there + 4)
        fraction_sent[there] = jnp.concatenate([static[0, part], static[1, part]], 0)
    fraction_got[gy] = fraction_sent[gy]

    pl.semaphore_wait(entry, DEVICES - 1)

    def send_first(there_x, there_y):
        pltpu.make_async_remote_copy(
            first_sent.at[there_x * GY + there_y],
            first_got.at[me],
            first_sem.at[0],
            first_sem.at[1],
            device_id=(there_x, there_y),
            device_id_type=MESH,
        ).start()

    to_others(send_first)

    def total(source, target, send, recv, rows):
        return pltpu.make_async_remote_copy(
            source.at[pl.ds(0, rows)],
            target.at[pl.ds(0, rows)],
            send,
            recv,
            device_id=(gx + 1 - 2 * core, gy),
            device_id_type=MESH,
        )

    offsets = sorted(
        [(dx, dy) for dx in range(4) for dy in range(2) if dx + dy > 0],
        key=lambda t: -(ring(t[0], 4) + 2 * t[1]),
    )
    peers = [lax.rem(x + dx, 4) * 2 + lax.rem(gy + dy, 2) for dx, dy in offsets]

    def to_peers(source, target, send, recv):
        for there in peers:
            pltpu.make_async_remote_copy(
                source.at[there],
                target.at[gy],
                send,
                recv,
                device_id=(gx, there),
                device_id_type=MESH,
            ).start()
        return total(source, target, send, recv, GY - 1)

    fraction_copies = to_peers(fraction_sent, fraction_got, fraction_sem.at[0], fraction_sem.at[1])

    for copy in inputs[3:]:
        copy.wait()
    for layer in range(2):
        static[2 + layer] = barrier[layer]
        static[4 + layer] = colour[layer].astype(F32)
        for section in range(SECTIONS):
            static[6 + 2 * section + layer] = direction[section, layer].astype(F32)
    upper = lax.broadcasted_iota(jnp.int32, (8, COLS), 0) < 4
    for kind in range(STATIC // 2):
        one, two = static[2 * kind], static[2 * kind + 1]
        rows_sent[0, kind] = jnp.where(upper, one[:8], pltpu.roll(two[:8], 4, 0))
        rows_sent[1, kind] = jnp.where(upper, pltpu.roll(one[-8:], 4, 0), two[-8:])
    flat = [static[k] for k in range(STATIC)] + [jnp.zeros((64, COLS), F32)]
    across = jnp.concatenate(flat, 0).T
    cols_sent[0] = across[:8]
    cols_sent[1] = across[-8:]

    up, down = lax.rem(gx + 1, GX), lax.rem(gx + GX - 1, GX)
    after, before = lax.rem(gy + 1, GY), lax.rem(gy + GY - 1, GY)
    halos = [
        (rows_sent.at[0], rows_got.at[0], (down, gy)),
        (rows_sent.at[1], rows_got.at[1], (up, gy)),
        (cols_sent.at[0], cols_got.at[0], (gx, before)),
        (cols_sent.at[1], cols_got.at[1], (gx, after)),
        (cols_sent.at[0], corner_got.at[0], (down, before)),
        (cols_sent.at[1], corner_got.at[1], (down, after)),
        (cols_sent.at[0], corner_got.at[2], (up, before)),
        (cols_sent.at[1], corner_got.at[3], (up, after)),
    ]
    halos = [
        pltpu.make_async_remote_copy(
            source, target, halo_send.at[k], halo_recv.at[k], device_id=there, device_id_type=MESH
        )
        for k, (source, target, there) in enumerate(halos)
    ]
    for copy in halos:
        copy.start()
    green_tables(me, green)

    total(first_sent, first_got, first_sem.at[0], first_sem.at[1], DEVICES - 1).wait_recv()
    received = jnp.concatenate([first_got[:, 0, :], first_got[:, 1, :]], 1)

    def start_exchange(slot, rows):
        packed[slot, :, 0, :] = rows

        def send(there_x, there_y):
            pltpu.make_async_remote_copy(
                packed.at[slot, there_x * GY + there_y],
                landed.at[slot, me],
                send_sem.at[slot],
                recv_sem.at[slot],
                device_id=(there_x, there_y),
                device_id_type=MESH,
            ).start()

        to_others(send)
        landed[slot, me] = packed[slot, me]

    def exchanged(slot):
        return total(
            packed.at[slot], landed.at[slot], send_sem.at[slot], recv_sem.at[slot], DEVICES - 1
        )

    def end_exchange(slot):
        exchanged(slot).wait_recv()
        return landed[slot, :, 0, :]

    start_exchange(0, spectral_first(received, coarse, back, turn, small, green))

    fraction_copies.wait_recv()
    pencil = jnp.concatenate([fraction_got[g] for g in range(GY)], 1)
    other = pltpu.roll(pencil, 4, 0)
    upper_wide = lax.broadcasted_iota(jnp.int32, (8, POINTS), 0) < 4
    fraction_pencil[0] = jnp.where(upper_wide, pencil, other)
    fraction_pencil[1] = jnp.where(upper_wide, other, pencil)
    for copy in halos:
        copy.wait_recv()

    def side(ahead, behind):
        gap = jnp.zeros((COLS - 16, 384), F32)
        return jnp.concatenate([ahead, gap, behind], 0).T

    beside = side(cols_got[0], cols_got[1])
    below = side(corner_got[0], corner_got[1])
    above = side(corner_got[2], corner_got[3])
    for k in range(STATIC):
        kind, layer = k // 2, k % 2
        part = slice(ROWS * k, ROWS * k + ROWS)
        fields[k, :ROWS, :COLS] = static[k]
        fields[k, :ROWS, COLS:] = beside[part]
        low, high = rows_got[0, kind], rows_got[1, kind]
        if layer == 0:
            high = pltpu.roll(high, 4, 0)
        else:
            low = pltpu.roll(low, 4, 0)
        fields[k, ROWS:, :COLS] = jnp.where(upper, low, high)
        fields[k, ROWS:, COLS:] = jnp.where(upper, below[part][:8], above[part][-8:])

    change = inverse_y(end_exchange(0), back, turn_y)
    for p in range(2):
        normal[p] = change[p][:8]
        shear[p] = change[p][8:]

    def sweep(i, carry):
        stress = []
        for p in range(2):
            stress_normal, stress_shear, _ = local_stress(normal[p], shear[p], fraction_pencil[p])
            stress.append(jnp.concatenate([stress_normal, stress_shear], 0))
        start_exchange(2 * i + 1, forward_y(stress, dft, turn_y))
        arrived = end_exchange(2 * i + 1)
        start_exchange(2 * i + 2, spectral(arrived, whole, back, turn, small, green))
        change = inverse_y(end_exchange(2 * i + 2), back, turn_y)
        for p in range(2):
            normal[p] += change[p][:8]
            shear[p] += change[p][8:]
        return carry

    for i in range(ITERS - 1):
        sweep(i, 0)

    energies = []
    for p in range(2):
        stress_normal, stress_shear, excess = local_stress(normal[p], shear[p], fraction_pencil[p])
        density = stress_normal * excess + 2.0 * stress_shear * shear[p]
        energies.append(0.5 * (density + pltpu.roll(density, 4, 0)))
    energy = jnp.where(upper_wide, energies[0], energies[1])
    shears = jnp.where(upper_wide, shear[0], pltpu.roll(shear[1], 4, 0))
    left = lax.broadcasted_iota(jnp.int32, (8, COLS), 1) < COLS // 2

    def block(values, g):
        return values[:, COLS * (g % GY) : COLS * (g % GY) + COLS]

    for g in range(GY):
        energy_sent[g, :, :COLS] = block(energy, g)
        energy_sent[g, :, COLS:] = jnp.where(left, block(energy, g + 1), block(energy, g - 1))

    def edge_copy(g, slot, there):
        return pltpu.make_async_remote_copy(
            energy_sent.at[g],
            energy_got.at[GY + slot],
            edge_send.at[slot],
            edge_recv.at[slot],
            device_id=(there, g),
            device_id_type=MESH,
        )

    @pl.when(gy == 0)
    def _():
        for g in range(GY):
            edge_copy(g, 0, down).start()

    @pl.when(gy == GY - 1)
    def _():
        for g in range(GY):
            edge_copy(g, 1, up).start()

    energy_copies = to_peers(energy_sent, energy_got, last_send.at[0], last_recv.at[0])
    for g in range(GY):
        strain_sent[g, 0:8] = block(normal[0], g)
        strain_sent[g, 8:16] = block(normal[1], g)
        strain_sent[g, 16:24] = block(shears, g)
    strain_copies = to_peers(strain_sent, strain_got, last_send.at[1], last_recv.at[1])
    energy_got[gy] = energy_sent[gy]
    strain_got[gy] = strain_sent[gy]

    total(first_sent, first_got, first_sem.at[0], first_sem.at[1], DEVICES - 1).wait_send()
    fraction_copies.wait_send()
    for copy in halos:
        copy.wait_send()
    for slot in range(2 * ITERS - 1):
        exchanged(slot).wait_send()

    low = lax.broadcasted_iota(jnp.int32, (8, 2 * COLS), 0) < 4
    tall, wide_cols = ROWS + 8, 2 * COLS

    def prepared(sites, layer, section):
        way = fields[6 + 2 * section + layer]
        above, below = pltpu.roll(sites, 1, 0), pltpu.roll(sites, tall - 1, 0)
        ahead, behind = pltpu.roll(sites, wide_cols - 1, 1), pltpu.roll(sites, 1, 1)
        neighbours = above + below + behind + ahead
        target = jnp.where(
            way == 0.0,
            below,
            jnp.where(way == 1.0, above, jnp.where(way == 2.0, ahead, behind)),
        )
        moving = jnp.where(
            fields[4 + layer] == float(section), sites * (1.0 - target), 0.0
        )
        return bond_energy * neighbours - (fields[2 + layer] + base_rate), moving

    def hop(sites, ready, energy, layer, section):
        flux = ready[1] / (1.0 + jnp.exp(ready[0] - elastic_weight * energy))
        way = fields[6 + 2 * section + layer]
        parted = [jnp.where(way == float(number), flux, 0.0) for number in range(4)]
        return (
            sites
            - flux
            + (
                pltpu.roll(parted[0], 1, 0)
                + pltpu.roll(parted[1], tall - 1, 0)
                + pltpu.roll(parted[2], 1, 1)
                + pltpu.roll(parted[3], wide_cols - 1, 1)
            )
        )

    ready = [prepared(fields[layer], layer, 0) for layer in range(2)]

    energy_copies.wait_recv()
    for slot in range(2):
        edge_copy(0, slot, up).wait_recv()

    for layer in range(2):
        pieces = []
        for pair in range(GY // 2 + 1):
            one, two = energy_got[2 * pair], energy_got[2 * pair + 1]
            if layer == 0:
                pieces.append(jnp.where(low, one, pltpu.roll(two, 4, 0)))
            else:
                pieces.append(jnp.where(low, pltpu.roll(one, 4, 0), two))
        energy_here = jnp.concatenate(pieces, 0)
        sites = hop(fields[layer], ready[layer], energy_here, layer, 0)
        for section in range(1, SECTIONS):
            sites = hop(sites, prepared(sites, layer, section), energy_here, layer, section)
        composition_out[layer] = sites[:ROWS, :COLS]

    strain_copies.wait_recv()
    for g in range(GY):
        rows = slice(4 * g, 4 * g + 4)
        for layer in range(2):
            strain_out[0, layer, rows] = strain_got[g, 8 * layer : 8 * layer + 4]
            strain_out[1, layer, rows] = strain_got[g, 8 * layer + 4 : 8 * layer + 8]
            strain_out[2, layer, rows] = strain_got[g, 16 + 4 * layer : 20 + 4 * layer]

    energy_copies.wait_send()
    strain_copies.wait_send()

    @pl.when(gy == 0)
    def _():
        for g in range(GY):
            edge_copy(g, 0, down).wait_send()

    @pl.when(gy == GY - 1)
    def _():
        for g in range(GY):
            edge_copy(g, 1, up).wait_send()


def on_device(occupancy, colour, hop_direction, barrier):
    operands = (occupancy, colour, hop_direction, barrier) + tuple(
        jnp.asarray(table) for table in tables()
    )
    vmem = pl.BlockSpec(memory_space=pltpu.VMEM)
    dma = pltpu.SemaphoreType.DMA
    exchanges = 2 * ITERS - 1
    return pl.pallas_call(
        kernel,
        out_shape=(
            jax.ShapeDtypeStruct((3, 2, ROWS, COLS), F32),
            jax.ShapeDtypeStruct((2, ROWS, COLS), F32),
        ),
        in_specs=[pl.BlockSpec(memory_space=pltpu.HBM)] * len(operands),
        out_specs=(vmem, vmem),
        scratch_shapes=[
            pltpu.VMEM((2, ROWS, COLS), jnp.int32),
            pltpu.VMEM((2, ROWS, COLS), jnp.int32),
            pltpu.VMEM((2, 2, ROWS, COLS), jnp.int32),
            pltpu.VMEM((2, ROWS, COLS), F32),
            pltpu.VMEM((1312, 256), BF16),
            pltpu.VMEM((512, 512), BF16),
            pltpu.VMEM((128, 896), BF16),
            pltpu.VMEM((4, 256, 128), F32),
            pltpu.VMEM((2, 64, 256), F32),
            pltpu.VMEM((2, 16, COLS), F32),
            pltpu.VMEM((3, 256, 128), F32),
            pltpu.VMEM((2, 8, POINTS), F32),
            pltpu.VMEM((2, 8, POINTS), F32),
            pltpu.VMEM((2, 8, POINTS), F32),
            pltpu.VMEM((DEVICES, 2, 128), F32),
            pltpu.VMEM((DEVICES, 2, 128), F32),
            pltpu.VMEM((exchanges, DEVICES, 1, 128), F32),
            pltpu.VMEM((exchanges, DEVICES, 1, 128), F32),
            pltpu.VMEM((GY, 8, COLS), F32),
            pltpu.VMEM((GY, 8, COLS), F32),
            pltpu.VMEM((STATIC, ROWS, COLS), F32),
            pltpu.VMEM((2, STATIC // 2, 8, COLS), F32),
            pltpu.VMEM((2, STATIC // 2, 8, COLS), F32),
            pltpu.VMEM((2, 8, 384), F32),
            pltpu.VMEM((2, 8, 384), F32),
            pltpu.VMEM((4, 8, 384), F32),
            pltpu.VMEM((STATIC, ROWS + 8, 2 * COLS), F32),
            pltpu.VMEM((GY, 24, COLS), F32),
            pltpu.VMEM((GY, 24, COLS), F32),
            pltpu.VMEM((GY, 8, 2 * COLS), F32),
            pltpu.VMEM((GY + 2, 8, 2 * COLS), F32),
            dma((10,)),
            dma((2,)),
            dma((exchanges,)),
            dma((exchanges,)),
            dma((2,)),
            dma((8,)),
            dma((8,)),
            dma((2,)),
            dma((2,)),
            dma((2,)),
            dma((2,)),
        ],
        compiler_params=pltpu.CompilerParams(
            collective_id=0, has_side_effects=True, vmem_limit_bytes=40 * 1024 * 1024
        ),
        name="film",
    )(*[pltpu.with_memory_space_constraint(x, pltpu.HBM) for x in operands])


def solution(mesh):
    placed = (
        P(None, "gx", "gy"),
        P(None, "gx", "gy"),
        P(None, None, "gx", "gy"),
        P(None, "gx", "gy"),
    )
    return jax.shard_map(
        on_device,
        mesh=mesh,
        in_specs=placed,
        out_specs=(P(None, None, "gx", "gy"), P(None, "gx", "gy")),
        check_vma=False,
    )
```
